32 devices in a mesh: dp: 8 (over z, y), expert: 4 (over x, core).
Axes of the slice: x: 2, y: 2, z: 4, core: 2. Of those that a mesh axis runs over, the one named last changes fastest.
Arguments:
- features: bfloat16 [16384, 80], P(('dp', 'expert')), may hold values from -6 to 6
- lengths: int32 [32, 4], P(('dp', 'expert')), may hold values from 0 to 512, as said below
- routes: int32 [2, 16384, 1], P(None, ('dp', 'expert')), may hold values from 0 to 3; in each aligned block of 512 rows (0 to 511, 512 to 1023, ..., all dimensions but the last counted through in order) at most 160 rows name the same one
- alignment: int32 [16384], P(('dp', 'expert')), may hold values from 0 to 8191
- attend_copy: bfloat16 [512, 1536], P('dp'), may hold values from -0.25 to 0.25
- output_copy: bfloat16 [512, 512], P('dp'), may hold values from -2 to 2
- conv_copy: bfloat16 [512, 1536], P('dp'), may hold values from -0.25 to 0.25
- head_copy: bfloat16 [512, 8192], P('dp'), may hold values from -0.5 to 0.5
- extra_copy: bfloat16 [512, 103], P('dp'), may hold values from -4 to 4
- gains_copy: bfloat16 [5, 512], P(None, 'dp'), may hold values from 0.3 to 2.5
- up_copy: bfloat16 [2, 4, 512, 2048], P(None, 'expert', 'dp'), may hold values from -0.25 to 0.25
- down_copy: bfloat16 [2, 4, 2048, 512], P(None, 'expert', None, 'dp'), may hold values from -1.5 to 1.5
- attend_master: float32 [512, 1536], P('dp'), may hold values from -0.25 to 0.25
- output_master: float32 [512, 512], P('dp'), may hold values from -2 to 2
- conv_master: float32 [512, 1536], P('dp'), may hold values from -0.25 to 0.25
- head_master: float32 [512, 8192], P('dp'), may hold values from -0.5 to 0.5
- extra_master: float32 [512, 103], P('dp'), may hold values from -0.625 to 0.625
- gains_master: float32 [5, 512], P(None, 'dp'), may hold values from 0.5 to 1.5
- up_master: float32 [2, 4, 512, 2048], P(None, 'expert', 'dp'), may hold values from -0.25 to 0.25
- down_master: float32 [2, 4, 2048, 512], P(None, 'expert', None, 'dp'), may hold values from -1.5 to 1.5
- attend_first: float32 [512, 1536], P('dp'), may hold values from -2.2888184e-05 to 2.2888184e-05
- output_first: float32 [512, 512], P('dp'), may hold values from -2.2888184e-05 to 2.2888184e-05
- conv_first: float32 [512, 1536], P('dp'), may hold values from -2.2888184e-05 to 2.2888184e-05
- head_first: float32 [512, 8192], P('dp'), may hold values from -2.2888184e-05 to 2.2888184e-05
- extra_first: float32 [512, 103], P('dp'), may hold values from -2.2888184e-05 to 2.2888184e-05
- gains_first: float32 [5, 512], P(None, 'dp'), may hold values from -9.1552734e-05 to 9.1552734e-05
- up_first: float32 [2, 4, 512, 2048], P(None, 'expert', 'dp'), may hold values from -2.2888184e-05 to 2.2888184e-05
- down_first: float32 [2, 4, 2048, 512], P(None, 'expert', None, 'dp'), may hold values from -5.722046e-06 to 5.722046e-06
- attend_second: float32 [512, 1536], P('dp'), may hold values from 6.8345377e-12 to 1.093526e-10
- output_second: float32 [512, 512], P('dp'), may hold values from 6.8345377e-12 to 1.093526e-10
- conv_second: float32 [512, 1536], P('dp'), may hold values from 6.8345377e-12 to 1.093526e-10
- head_second: float32 [512, 8192], P('dp'), may hold values from 6.8345377e-12 to 1.093526e-10
- extra_second: float32 [512, 103], P('dp'), may hold values from 6.8345377e-12 to 1.093526e-10
- gains_second: float32 [5, 512], P(None, 'dp'), may hold values from 1.093526e-10 to 1.7496417e-09
- up_second: float32 [2, 4, 512, 2048], P(None, 'expert', 'dp'), may hold values from 6.8345377e-12 to 1.093526e-10
- down_second: float32 [2, 4, 2048, 512], P(None, 'expert', None, 'dp'), may hold values from 4.271586e-13 to 6.8345377e-12
Outputs:
- loss_sum: float32 [], replicated
- frame_count: float32 [], replicated
- grad_norm: float32 [], replicated
- attend_moment: float32 [512, 1536], P('dp')
- output_moment: float32 [512, 512], P('dp')
- conv_moment: float32 [512, 1536], P('dp')
- head_moment: float32 [512, 8192], P('dp')
- extra_moment: float32 [512, 103], P('dp')
- gains_moment: float32 [5, 512], P(None, 'dp')
- up_moment: float32 [2, 4, 512, 2048], P(None, 'expert', 'dp')
- down_moment: float32 [2, 4, 2048, 512], P(None, 'expert', None, 'dp')
- attend_square: float32 [512, 1536], P('dp')
- output_square: float32 [512, 512], P('dp')
- conv_square: float32 [512, 1536], P('dp')
- head_square: float32 [512, 8192], P('dp')
- extra_square: float32 [512, 103], P('dp')
- gains_square: float32 [5, 512], P(None, 'dp')
- up_square: float32 [2, 4, 512, 2048], P(None, 'expert', 'dp')
- down_square: float32 [2, 4, 2048, 512], P(None, 'expert', None, 'dp')
- attend_new: float32 [512, 1536], P('dp')
- output_new: float32 [512, 512], P('dp')
- conv_new: float32 [512, 1536], P('dp')
- head_new: float32 [512, 8192], P('dp')
- extra_new: float32 [512, 103], P('dp')
- gains_new: float32 [5, 512], P(None, 'dp')
- up_new: float32 [2, 4, 512, 2048], P(None, 'expert', 'dp')
- down_new: float32 [2, 4, 2048, 512], P(None, 'expert', None, 'dp')
The draws below stay inside these ranges and needn't reach their ends.
Inputs may be any that keep to these rules, and one draw needn't show every extreme that they name: `lengths`: each row has 3 utterances of one frame or more followed by padding of zero frames or more; a row sums to 512. `routes`: among the frames of one row, no expert of one feed-forward is named by more than 160 frames, and 160 is reached.
All inputs are finite; a program needn't handle non-finite values.
Results may differ from the reference program's by a relative error of at most 0.03.
Values may be sent and summed in bfloat16 or wider, within the bound.
No kernel may reach another device: no remote copies, remote signals or barrier semaphores. Data moves between devices by JAX's collectives and lax.ppermute only.
A program may use at most 256 MiB of HBM per device.

```python
import math
import jax
import jax.numpy as jnp
import numpy as np
from jax import lax

D = 512
HEADS = 8
HEAD = 64
FF = 2048
FEAT = 80
V = 8192
KERNEL = 15
SEGS = 4
EXP_DEV = 1
STEP = 5
ROW = 512
ROWS = 32
TOKENS = 16384
E = 4
CAP = 160
AUX = 103
PARAMS = 22861824


def draw_lengths(key, part):
    key = jax.random.fold_in(key, 7)
    expert_count = E // EXP_DEV
    dp_count = ROWS // expert_count
    row_index = jnp.arange(ROWS, dtype=jnp.int32)
    dp_place = row_index // expert_count
    expert_place = row_index % expert_count
    weight = (dp_count - 1 + 2 * dp_place) * (expert_count - 1 + 2 * expert_place)
    ceiling = 9 * (dp_count - 1) * (expert_count - 1)
    first_key, second_key = jax.random.split(key)
    jitter = jax.random.randint(first_key, (ROWS,), 0, ROW // 32 + 1)
    live_frames = jnp.clip(ROW * weight // ceiling - jitter, 4 * (SEGS - 1), ROW)
    shares_drawn = jax.random.randint(second_key, (ROWS, SEGS - 1), 1, 17)
    spare_frames = live_frames - (SEGS - 1)
    utterances = 1 + spare_frames[:, None] * shares_drawn // jnp.sum(shares_drawn, axis=1, keepdims=True)
    utterances = utterances.at[:, -1].add(live_frames - jnp.sum(utterances, axis=1))
    return jnp.concatenate([utterances, (ROW - live_frames)[:, None]], axis=1).astype(jnp.int32)


def draw_extra_copy(key, part):
    key = jax.random.fold_in(key, 5)
    column = jnp.arange(AUX)
    column_scale = jnp.where(column < 2 * E, 0.6 * D ** (-0.5), jnp.where(column < 2 * E + FEAT, FEAT ** (-0.5), 2.0 * KERNEL ** (-0.5)))
    entries = jnp.clip(jax.random.normal(key, (D, AUX), jnp.float32), -6.0, 6.0)
    return (entries * column_scale).astype(jnp.bfloat16)


def draw_gains_copy(key, part):
    key = jax.random.fold_in(key, 11)
    ramp = jnp.arange(D, dtype=jnp.float32) / (D - 1)
    rising = 0.5 * (1.0 + 2.0 * ramp)
    jiggle = jax.random.uniform(key, (5, D), jnp.float32, 0.8, 1.2)
    return (rising[None, :] * jiggle).astype(jnp.bfloat16)


def plant(array, stream_key, smallest, top_value):
    longest = array.shape.index(max(array.shape))
    spots = []
    for shift in (0, 1):
        where = [jax.random.randint(jax.random.fold_in(stream_key, axis), (), 0, length) for axis, length in enumerate(array.shape)]
        where[longest] = (where[longest] + shift) % array.shape[longest]
        spots.append(tuple(where))
    return array.at[spots[0]].set(smallest).at[spots[1]].set(top_value)


def block_scale(rng, shape, cuts, low, top_value):
    def one(axis_at, blocks):
        draws = jax.random.uniform(jax.random.fold_in(jax.random.fold_in(rng, 6), axis_at), (blocks,), jnp.float32, low / len(cuts), top_value / len(cuts))
        return jnp.repeat(jnp.exp(draws), shape[axis_at] // blocks).reshape((-1,) + (1,) * (len(shape) - axis_at - 1))

    loudness = one(*cuts[0])
    for cut in cuts[1:]:
        loudness = loudness * one(*cut)
    return loudness


def routed_block(key, own, number, rows, number_of, top, limit, slope):
    sequence = jax.random.permutation(key, number_of)
    heavy_load, ordinary = portions_of(number_of, rows * top, limit, slope, True), portions_of(number_of, rows * top, limit, slope, False)
    places = jnp.arange(number_of)

    def named(sizes, rotation):
        used = int((sizes > 0).sum())
        fixed = max(1, used // 4)
        shifted = fixed + (places - fixed + rotation * (used - fixed)) % max(1, number_of - fixed)
        return jnp.zeros((number_of,), jnp.int32).at[sequence[jnp.where(places < fixed, places, shifted)]].set(jnp.asarray(sizes, jnp.int32))

    sizes = jnp.where(number % 4 == 0, named(heavy_load, number // 4), named(ordinary, number - number // 4 - 1))
    mixed = jax.random.permutation(jax.random.fold_in(own, 3), number_of)
    donor, receiver = mixed[0:number_of // 2 * 2:2], mixed[1:number_of // 2 * 2:2]
    margin = jnp.minimum(sizes[donor] - 1, limit - sizes[receiver]) // 2
    margin = jnp.where((donor == sequence[0]) | (receiver == sequence[0]) | (sizes[receiver] == 0), 0, jnp.maximum(margin, 0))
    shifted = jax.random.randint(jax.random.fold_in(own, 4), (number_of // 2,), 0, 1 << 20) % (margin + 1)
    sizes = sizes.at[donor].add(-shifted).at[receiver].add(shifted)
    labels = jnp.searchsorted(jnp.cumsum(sizes), jnp.arange(rows * top), side="right").astype(jnp.int32)
    grid = labels.reshape(top, rows).T
    grid = grid[jax.random.permutation(jax.random.fold_in(own, 1), rows)]
    rotation = jax.random.randint(jax.random.fold_in(own, 2), (rows, 1), 0, top)
    return jnp.take_along_axis(grid, (jnp.arange(top)[None, :] + rotation) % top, axis=1)


def portions_of(number_of, total, most, lean, full):
    weights = [(1 << 20) // math.isqrt(standing ** lean) + 1 for standing in range(1, number_of + 1)]
    largest = most if full else min(most, max(-(-total // number_of), total * weights[0] // sum(weights)))
    least = 1 if total - largest >= number_of - 1 else 0
    counts, surplus = [largest] + [least] * (number_of - 1), total - largest - least * (number_of - 1)
    while surplus > 0:
        candidates = [i for i in range(1, number_of) if counts[i] < largest] or [i for i in range(1, number_of) if counts[i] < most]
        whole, remaining = sum([weights[i] for i in candidates]), surplus
        for i in candidates:
            addition = min(most - counts[i], max(1, remaining * weights[i] // whole), surplus)
            counts[i] = counts[i] + addition
            surplus = surplus - addition
    return np.array(counts)


def gaussian(rng, extent, scale, reach, pieces=(), kind=jnp.bfloat16):
    result = jax.random.normal(rng, extent, jnp.float32) * scale
    if len(pieces) > 0:
        result = block_scale(rng, extent, pieces, -0.22, 0.18) * result
    return jnp.clip(result, min=-reach, max=reach).astype(kind)


def setup_inputs(seed: int = 0) -> dict:
    key_list = jax.random.split(jax.random.key(seed), 37)
    features = gaussian(key_list[0], (TOKENS, FEAT), 1.0, 6.0, ((0, 32),))
    lengths = draw_lengths(jax.random.fold_in(key_list[36], 71), 0)
    routes_keys = jax.random.split(jax.random.fold_in(key_list[2], 1), 2 * TOKENS // ROW)
    routes_turns = jax.random.permutation(jax.random.fold_in(key_list[2], 3), 2 * TOKENS // ROW)
    routes = jax.vmap(lambda own, number: routed_block(jax.random.fold_in(key_list[2], 2), own, number, ROW, E, 1, CAP, 1))(routes_keys, routes_turns).reshape((2, TOKENS, 1))
    alignment = plant(jax.random.randint(key_list[3], (TOKENS,), 0, V), jax.random.fold_in(key_list[3], 1), 0, V - 1).astype(jnp.int32)
    attend_copy = gaussian(key_list[4], (D, 3 * D), D ** -0.5, 0.25, ((0, 8),))
    output_copy = gaussian(key_list[5], (D, D), (D * 7 // ROW) ** -0.5, 2.0, ((0, 8),))
    conv_copy = gaussian(key_list[6], (D, 3 * D), D ** -0.5, 0.25, ((0, 8),))
    head_copy = gaussian(key_list[7], (D, V), (D // 4) ** -0.5, 0.5, ((0, 8),))
    extra_copy = draw_extra_copy(jax.random.fold_in(key_list[36], 71), 0)
    gains_copy = draw_gains_copy(jax.random.fold_in(key_list[36], 71), 0)
    up_copy = gaussian(key_list[10], (2, E, D, FF), D ** -0.5, 0.25, ((1, 4), (2, 8)))
    down_copy = gaussian(key_list[11], (2, E, FF, D), (max(FF // 128, 1)) ** -0.5, 1.5, ((1, 4), (3, 8)))
    attend_master = gaussian(key_list[12], (D, 3 * D), D ** -0.5, 0.25, ((0, 8),), jnp.float32)
    output_master = gaussian(key_list[13], (D, D), (D * 7 // ROW) ** -0.5, 2.0, ((0, 8),), jnp.float32)
    conv_master = gaussian(key_list[14], (D, 3 * D), D ** -0.5, 0.25, ((0, 8),), jnp.float32)
    head_master = gaussian(key_list[15], (D, V), (D // 4) ** -0.5, 0.5, ((0, 8),), jnp.float32)
    extra_master = gaussian(key_list[16], (D, AUX), FEAT ** -0.5, 0.625, ((0, 8),), jnp.float32)
    gains_master = jnp.clip(1.0 + 0.1 * jax.random.normal(key_list[17], (5, D), jnp.float32), 0.5, 1.5)
    up_master = gaussian(key_list[18], (2, E, D, FF), D ** -0.5, 0.25, ((1, 4), (2, 8)), jnp.float32)
    down_master = gaussian(key_list[19], (2, E, FF, D), (max(FF // 128, 1)) ** -0.5, 1.5, ((1, 4), (3, 8)), jnp.float32)
    attend_first = gaussian(key_list[20], (D, 3 * D), ((0.01 * D / (TOKENS * PARAMS)) ** 0.5), 2.288818359375e-05, ((0, 8),), jnp.float32)
    output_first = gaussian(key_list[21], (D, D), ((0.01 * D / (TOKENS * PARAMS)) ** 0.5), 2.288818359375e-05, ((0, 8),), jnp.float32)
    conv_first = gaussian(key_list[22], (D, 3 * D), ((0.01 * D / (TOKENS * PARAMS)) ** 0.5), 2.288818359375e-05, ((0, 8),), jnp.float32)
    head_first = gaussian(key_list[23], (D, V), ((0.01 * D / (TOKENS * PARAMS)) ** 0.5), 2.288818359375e-05, ((0, 8),), jnp.float32)
    extra_first = gaussian(key_list[24], (D, AUX), ((0.01 * D / (TOKENS * PARAMS)) ** 0.5), 2.288818359375e-05, ((0, 8),), jnp.float32)
    gains_first = gaussian(key_list[25], (5, D), (4 * (0.01 * D / (TOKENS * PARAMS)) ** 0.5), 9.1552734375e-05, ((1, 8),), jnp.float32)
    up_first = gaussian(key_list[26], (2, E, D, FF), ((0.01 * D / (TOKENS * PARAMS)) ** 0.5), 2.288818359375e-05, ((1, 4), (2, 8)), jnp.float32)
    down_first = gaussian(key_list[27], (2, E, FF, D), (0.025 * (FF / (4 * TOKENS * PARAMS)) ** 0.5), 5.7220458984375e-06, ((1, 4), (3, 8)), jnp.float32)
    attend_second = jnp.clip(jnp.exp(math.log(1.0935260336131236e-10) - 2.7725887 * jax.random.uniform(key_list[28], (D, 3 * D), jnp.float32) ** block_scale(key_list[28], (D, 3 * D), ((0, 8),), -0.2, 0.2)), 6.834537710082023e-12, 1.0935260336131236e-10)
    output_second = jnp.clip(jnp.exp(math.log(1.0935260336131236e-10) - 2.7725887 * jax.random.uniform(key_list[29], (D, D), jnp.float32) ** block_scale(key_list[29], (D, D), ((0, 8),), -0.2, 0.2)), 6.834537710082023e-12, 1.0935260336131236e-10)
    conv_second = jnp.clip(jnp.exp(math.log(1.0935260336131236e-10) - 2.7725887 * jax.random.uniform(key_list[30], (D, 3 * D), jnp.float32) ** block_scale(key_list[30], (D, 3 * D), ((0, 8),), -0.2, 0.2)), 6.834537710082023e-12, 1.0935260336131236e-10)
    head_second = jnp.clip(jnp.exp(math.log(1.0935260336131236e-10) - 2.7725887 * jax.random.uniform(key_list[31], (D, V), jnp.float32) ** block_scale(key_list[31], (D, V), ((0, 8),), -0.2, 0.2)), 6.834537710082023e-12, 1.0935260336131236e-10)
    extra_second = jnp.clip(jnp.exp(math.log(1.0935260336131236e-10) - 2.7725887 * jax.random.uniform(key_list[32], (D, AUX), jnp.float32) ** block_scale(key_list[32], (D, AUX), ((0, 8),), -0.2, 0.2)), 6.834537710082023e-12, 1.0935260336131236e-10)
    gains_second = jnp.clip(jnp.exp(math.log(1.7496416537809978e-09) - 2.7725887 * jax.random.uniform(key_list[33], (5, D), jnp.float32) ** block_scale(key_list[33], (5, D), ((1, 8),), -0.2, 0.2)), 1.0935260336131236e-10, 1.7496416537809978e-09)
    up_second = jnp.clip(jnp.exp(math.log(1.0935260336131236e-10) - 2.7725887 * jax.random.uniform(key_list[34], (2, E, D, FF), jnp.float32) ** block_scale(key_list[34], (2, E, D, FF), ((1, 4), (2, 8)), -0.2, 0.2)), 6.834537710082023e-12, 1.0935260336131236e-10)
    down_second = jnp.clip(jnp.exp(math.log(6.834537710082023e-12) - 2.7725887 * jax.random.uniform(key_list[35], (2, E, FF, D), jnp.float32) ** block_scale(key_list[35], (2, E, FF, D), ((1, 4), (3, 8)), -0.2, 0.2)), 4.271586068801264e-13, 6.834537710082023e-12)
    return dict(features=features, lengths=lengths, routes=routes, alignment=alignment, attend_copy=attend_copy, output_copy=output_copy, conv_copy=conv_copy, head_copy=head_copy, extra_copy=extra_copy, gains_copy=gains_copy, up_copy=up_copy, down_copy=down_copy, attend_master=attend_master, output_master=output_master, conv_master=conv_master, head_master=head_master, extra_master=extra_master, gains_master=gains_master, up_master=up_master, down_master=down_master, attend_first=attend_first, output_first=output_first, conv_first=conv_first, head_first=head_first, extra_first=extra_first, gains_first=gains_first, up_first=up_first, down_first=down_first, attend_second=attend_second, output_second=output_second, conv_second=conv_second, head_second=head_second, extra_second=extra_second, gains_second=gains_second, up_second=up_second, down_second=down_second)


NORM_EPS = 1e-05
ADAM_EPS = 1e-08
BETA_ONE = 0.5
BETA_TWO = 0.5
MASKED = -1000000000.0
GROUP_ROWS = 8
STEP_RATES = (0.02, 0.2, 0.02, 0.05, 0.05, 0.5, 0.02, 0.1)
DECAYS = (0.01, 0.01, 0.01, 0.01, 0.01, 0.0, 0.01, 0.01)
HIGHEST = lax.Precision.HIGHEST

@jax.custom_vjp
def low(v):
    return lax.optimization_barrier(v.astype(jnp.bfloat16)).astype(jnp.float32)

@jax.custom_vjp
def low_back(v):
    return v

def low_keep(v):
    return (low(v), None)

def low_pass(kept, grad):
    return (grad,)

def back_keep(v):
    return (v, None)

def back_low(kept, grad):
    return (low(grad),)
low.defvjp(low_keep, low_pass)
low_back.defvjp(back_keep, back_low)

def matmul(left_side, right_side):
    return jnp.matmul(left_side, right_side, precision=HIGHEST)

def layer_norm(values, gain_row):
    centred = values - lax.optimization_barrier(jnp.mean(values, axis=-1, keepdims=True))
    spread = lax.optimization_barrier(jnp.mean(centred * centred, axis=-1, keepdims=True))
    return centred * lax.rsqrt(spread + NORM_EPS) * gain_row

def segment_ids(lengths):
    bounds = jnp.cumsum(lengths[:, :SEGS - 1], axis=1).astype(jnp.int32)
    places = jnp.arange(ROW, dtype=jnp.int32)
    segment = lax.optimization_barrier(jnp.sum((places[None, :, None] >= bounds[:, None, :]).astype(jnp.int32), axis=-1)).astype(jnp.int32)
    counted = (places[None, :] < bounds[:, -1:]).astype(jnp.float32)
    return (segment, counted)

def grouped(function, *arrays):
    shaped = tuple((member.reshape((ROWS // GROUP_ROWS, GROUP_ROWS) + member.shape[1:]) for member in arrays))
    return lax.map(jax.checkpoint(lambda batch: function(*batch)), shaped)

def attention(hidden, segment, attend, output, gain_row):
    normed = low(layer_norm(hidden, gain_row))
    packed = low(low_back(matmul(normed, attend)))
    head_shape = hidden.shape[:-1] + (HEADS, HEAD)
    queries = packed[..., :D].reshape(head_shape)
    key_rows = packed[..., D:2 * D].reshape(head_shape)
    values = packed[..., 2 * D:].reshape(head_shape)
    scores = low_back(jnp.einsum('gqhd,gkhd->ghqk', queries, key_rows, precision=HIGHEST) * HEAD ** (-0.5))
    same_segment = (segment[:, :, None] == segment[:, None, :])[:, None]
    scores = jnp.where(same_segment, scores, MASKED)
    weights = low(jax.nn.softmax(scores, axis=-1))
    blended = low(low_back(jnp.einsum('ghqk,gkhd->gqhd', weights, values, precision=HIGHEST)))
    return low_back(matmul(blended.reshape(hidden.shape), output))

def convolve(hidden, segment, conv_weight, depth_kernel, gain_row):
    normed = low(layer_norm(hidden, gain_row))
    projected = low_back(matmul(normed, conv_weight[:, :2 * D]))
    gated_half = projected[..., :D] * jax.nn.sigmoid(projected[..., D:])
    half_span = KERNEL // 2
    padded = jnp.pad(gated_half, ((0, 0), (half_span, half_span), (0, 0)))
    padded_ids = jnp.pad(segment, ((0, 0), (half_span, half_span)), constant_values=-1)
    totals = jnp.zeros_like(gated_half)
    for offset in range(KERNEL):
        same_segment = (padded_ids[:, offset:offset + ROW] == segment)[..., None]
        totals = totals + jnp.where(same_segment, padded[:, offset:offset + ROW], 0.0) * depth_kernel[:, offset]
    blended = low(jax.nn.silu(totals))
    return low_back(matmul(blended, conv_weight[:, 2 * D:]))

def expert_block(batch):
    slot_rows, up_block, down_block = batch
    hidden = low_back(jnp.einsum('nd,df->nf', slot_rows, up_block, precision=HIGHEST))
    activated = low(jax.nn.silu(hidden))
    return low(low_back(jnp.einsum('nf,fd->nd', activated, down_block, precision=HIGHEST)))

def slot_places(route_ids):
    chosen_mask = (route_ids[:, None] == jnp.arange(E, dtype=jnp.int32)[None, :]).astype(jnp.int32)
    blocks = chosen_mask.reshape(ROWS, ROW, E)
    slot_rank = lax.optimization_barrier(jnp.sum((jnp.cumsum(blocks, axis=1).astype(jnp.int32) - blocks) * blocks, axis=-1)).astype(jnp.int32)
    device_rows = jnp.arange(TOKENS, dtype=jnp.int32) // ROW
    slot_index = (device_rows * E + route_ids) * CAP + slot_rank.reshape(TOKENS)
    source = jnp.full((ROWS * E * CAP,), TOKENS, jnp.int32).at[slot_index].set(jnp.arange(TOKENS, dtype=jnp.int32))
    return (slot_index, source)

def mixture(hidden, route_ids, router, up_block, down_block, gain_row):
    normed = low(layer_norm(hidden, gain_row))
    logits = low_back(matmul(normed, router))
    router_prob = jax.nn.softmax(logits, axis=-1)
    chosen_mask = route_ids[:, None] == jnp.arange(E, dtype=jnp.int32)[None, :]
    gate_prob = lax.optimization_barrier(jnp.sum(jnp.where(chosen_mask, router_prob, 0.0), axis=-1))
    slot_index, source = slot_places(route_ids)
    padded = jnp.concatenate([normed, jnp.zeros((1, D), jnp.float32)], axis=0)
    slot_rows = low_back(padded[source])
    slot_rows = slot_rows.reshape(ROWS, E, CAP, D).transpose(1, 0, 2, 3).reshape(E, ROWS * CAP, D)
    expert_out = lax.map(jax.checkpoint(expert_block), (slot_rows, up_block, down_block))
    expert_out = expert_out.reshape(E, ROWS, CAP, D).transpose(1, 0, 2, 3).reshape(ROWS * E * CAP, D)
    return gate_prob[:, None] * expert_out[slot_index]

def forward(weights, features, segment, counted, routes, alignment):
    attend, output, conv_weight, head_weight, extra, gains, up_weight, down_weight = weights
    embedding = extra[:, 2 * E:2 * E + FEAT]
    depth_kernel = extra[:, 2 * E + FEAT:]
    embedded = low_back(matmul(features, embedding.T))
    after_one = embedded + 0.5 * mixture(embedded, routes[0, :, 0], extra[:, :E], up_weight[0], down_weight[0], gains[0])

    def middle(hidden, segment_rows):
        after_attend = hidden + attention(hidden, segment_rows, attend, output, gains[1])
        return after_attend + convolve(after_attend, segment_rows, conv_weight, depth_kernel, gains[2])
    after_conv = grouped(middle, after_one.reshape(ROWS, ROW, D), segment).reshape(TOKENS, D)
    after_two = after_conv + 0.5 * mixture(after_conv, routes[1, :, 0], extra[:, E:2 * E], up_weight[1], down_weight[1], gains[3])

    def losses(hidden, counted_rows, target_rows):
        normed = low(layer_norm(hidden, gains[4]))
        logits = low_back(matmul(normed, head_weight))
        log_total = jax.nn.logsumexp(logits, axis=-1)
        picked = jnp.take_along_axis(logits, target_rows[..., None], axis=-1)[..., 0]
        return jnp.sum((log_total - picked) * counted_rows)
    return jnp.sum(grouped(losses, after_two.reshape(ROWS, ROW, D), counted, alignment.reshape(ROWS, ROW)))

def adamw(gradient, master, moment, square, rate, decay):
    moment = BETA_ONE * moment + (1.0 - BETA_ONE) * gradient
    square = BETA_TWO * square + (1.0 - BETA_TWO) * gradient * gradient
    update = moment / (1.0 - BETA_ONE ** STEP) / (jnp.sqrt(square / (1.0 - BETA_TWO ** STEP)) + ADAM_EPS)
    return (moment, square, master - rate * (update + decay * master))

def reference(features, lengths, routes, alignment, attend_copy, output_copy, conv_copy, head_copy, extra_copy, gains_copy, up_copy, down_copy, attend_master, output_master, conv_master, head_master, extra_master, gains_master, up_master, down_master, attend_first, output_first, conv_first, head_first, extra_first, gains_first, up_first, down_first, attend_second, output_second, conv_second, head_second, extra_second, gains_second, up_second, down_second):
    copies = (attend_copy, output_copy, conv_copy, head_copy, extra_copy, gains_copy, up_copy, down_copy)
    masters = (attend_master, output_master, conv_master, head_master, extra_master, gains_master, up_master, down_master)
    moments = (attend_first, output_first, conv_first, head_first, extra_first, gains_first, up_first, down_first)
    squares = (attend_second, output_second, conv_second, head_second, extra_second, gains_second, up_second, down_second)
    params = tuple((member.astype(jnp.float32) for member in copies))
    segment, counted = segment_ids(lengths)
    wide_features = features.astype(jnp.float32)
    loss_sum, pull = jax.vjp(lambda *weights: forward(weights, wide_features, segment, counted, routes, alignment), *params)
    frame_count = jnp.sum(counted)
    gradients = pull(jnp.float32(1.0) / frame_count)
    squared = jnp.float32(0.0)
    for member in gradients:
        squared = squared + jnp.sum(member * member)
    grad_norm = jnp.sqrt(squared)
    factor = jnp.minimum(1.0, 0.1 * math.sqrt(D / TOKENS) / grad_norm)
    results = [adamw(gradient * factor, master, moment, square, rate, decay) for gradient, master, moment, square, rate, decay in zip(gradients, masters, moments, squares, STEP_RATES, DECAYS)]
    return (loss_sum, frame_count, grad_norm, results[0][0], results[1][0], results[2][0], results[3][0], results[4][0], results[5][0], results[6][0], results[7][0], results[0][1], results[1][1], results[2][1], results[3][1], results[4][1], results[5][1], results[6][1], results[7][1], results[0][2], results[1][2], results[2][2], results[3][2], results[4][2], results[5][2], results[6][2], results[7][2])
```

```python
import functools
import math

import jax
import jax.numpy as jnp
import numpy as np
from jax import lax
from jax.experimental import pallas as pl
from jax.experimental.pallas import tpu as pltpu
from jax.sharding import PartitionSpec as P

HEADS = 8
STEP = 5
NORM_EPS = 1e-05
ADAM_EPS = 1e-08
BETA_ONE = 0.5
BETA_TWO = 0.5
MASKED = -1000000000.0
STEP_RATES = (0.02, 0.2, 0.02, 0.05, 0.05, 0.5, 0.02, 0.1)
DECAYS = (0.01, 0.01, 0.01, 0.01, 0.01, 0.0, 0.01, 0.01)

BF = jnp.bfloat16
F32 = jnp.float32
ALL = ("dp", "expert")
VMEM_BYTES = 56 * 1024 * 1024
LANES = 128
TAP_PAD = 16


def nn(left, right):
    return jnp.dot(left, right, preferred_element_type=F32)


def nt(left, right):
    return lax.dot_general(left, right, (((1,), (1,)), ((), ())), preferred_element_type=F32)


def tn(left, right):
    return lax.dot_general(left, right, (((0,), (0,)), ((), ())), preferred_element_type=F32)


def norm_parts(values):
    centred = values - jnp.mean(values, axis=-1, keepdims=True)
    scale = lax.rsqrt(jnp.mean(centred * centred, axis=-1, keepdims=True) + NORM_EPS)
    return centred * scale, scale


def norm_back(grad, unit, scale, gain_row):
    weighted = grad * gain_row
    mean = jnp.mean(weighted, axis=-1, keepdims=True)
    along = jnp.mean(weighted * unit, axis=-1, keepdims=True)
    gain_grad = jnp.sum(grad * unit, axis=0, keepdims=True)
    return scale * (weighted - mean - unit * along), gain_grad


def lane_softmax(logits, first, count):
    lane = lax.broadcasted_iota(jnp.int32, logits.shape, 1)
    inside = (lane >= first) & (lane < first + count)
    logits = jnp.where(inside, logits, -jnp.inf)
    weight = jnp.exp(logits - jnp.max(logits, axis=-1, keepdims=True))
    return weight / jnp.sum(weight, axis=-1, keepdims=True)


def chosen_lanes(route_col, first, shape):
    lane = lax.broadcasted_iota(jnp.int32, shape, 1)
    return lane == (route_col.astype(jnp.int32) + first)


def bounds_of(lengths_ref):
    first = lengths_ref[0, 0]
    second = first + lengths_ref[0, 1]
    return first, second, second + lengths_ref[0, 2]


def segment_of(places, bounds):
    total = jnp.zeros(places.shape, jnp.int32)
    for bound in bounds:
        total = total + (places >= bound).astype(jnp.int32)
    return total


def tap_masks(rows, half_span, bounds):
    place = lax.broadcasted_iota(jnp.int32, (rows, LANES), 0)
    lane = lax.broadcasted_iota(jnp.int32, (rows, LANES), 1)
    same = segment_of(place, bounds) == segment_of(place + lane - half_span, bounds)
    return same.astype(F32)


def start_copies(pairs, sems):
    copies = [pltpu.make_async_copy(src, dst, sems.at[i]) for i, (src, dst) in enumerate(pairs)]
    for copy in copies:
        copy.start()
    return copies


def rows_at(rank, rows):
    return pl.ds(pl.multiple_of(rank * rows, rows), rows)


def shared_pairs(mine_ref, other_ref, full_ref, ranks_ref, core, steps, rows):
    width = mine_ref.shape[-1]
    own = pl.ds(pl.multiple_of(core * width, LANES), width)
    far = pl.ds(pl.multiple_of((1 - core) * width, LANES), width)
    pairs = []
    for k in range(steps):
        pairs.append((mine_ref.at[k], full_ref.at[rows_at(ranks_ref[0, k], rows), own]))
        pairs.append((other_ref.at[k], full_ref.at[rows_at(ranks_ref[1, k], rows), far]))
    return pairs


def shared_out_pairs(full_ref, mine_ref, other_ref, ranks_ref, core, steps, rows):
    width = mine_ref.shape[-1]
    own = pl.ds(pl.multiple_of(core * width, LANES), width)
    far = pl.ds(pl.multiple_of((1 - core) * width, LANES), width)
    pairs = []
    for k in range(steps):
        later = (k + 1) % steps
        pairs.append((full_ref.at[rows_at(ranks_ref[0, later], rows), own], mine_ref.at[k]))
        pairs.append((full_ref.at[rows_at(ranks_ref[1, later], rows), far], other_ref.at[k]))
    return pairs


def routing_kernel(capacity, routes_ref, align_ref, cols_ref, *place_refs):
    rows = routes_ref.shape[2]
    before = (
        lax.broadcasted_iota(jnp.int32, (rows, rows), 0)
        < lax.broadcasted_iota(jnp.int32, (rows, rows), 1)
    ).astype(BF)
    kept = []
    slots = []
    for f in range(2):
        route_row = routes_ref[f]
        named = lax.broadcasted_iota(jnp.int32, (16, rows), 0) == route_row
        counts = nn(named.astype(BF), before)
        rank = jnp.sum(jnp.where(named, counts, 0.0), axis=0, keepdims=True)
        slots.append(route_row.astype(F32) * capacity + rank)
        kept.append(route_row.astype(F32))
    lines = jnp.concatenate(
        kept + [align_ref[...].astype(F32)] + slots + [jnp.zeros((LANES - 5, rows), F32)], axis=0
    )
    cols = lines.T
    cols_ref[...] = cols
    for f in range(2):
        down_ref, across_ref = place_refs[2 * f], place_refs[2 * f + 1]
        slot_count = down_ref.shape[0]
        slot_row = slots[f].astype(jnp.int32)
        slot_col = cols[:, 3 + f : 4 + f].astype(jnp.int32)
        down_ref[...] = (
            lax.broadcasted_iota(jnp.int32, (slot_count, rows), 0) == slot_row
        ).astype(BF)
        across_ref[...] = (
            lax.broadcasted_iota(jnp.int32, (rows, slot_count), 1) == slot_col
        ).astype(BF)


def front_kernel(experts, feat_ref, extra_ref, place_ref, gain_at, x0_ref, slots_ref, prob_ref, lines_ref):
    extra = extra_ref[...]
    lines_ref[...] = extra.astype(F32).T
    feats = feat_ref.shape[0]
    table = lines_ref[2 * experts : 2 * experts + feats, :].astype(BF)
    embedded = tn(feat_ref[...], table)
    x0_ref[...] = embedded
    unit, _ = norm_parts(embedded)
    low = (unit * lines_ref[gain_at : gain_at + 1, :]).astype(BF)
    prob_ref[...] = lane_softmax(nn(low, extra), 0, experts)
    slots_ref[...] = nn(place_ref[...], low).astype(BF)


def load_experts(ranks_ref, chunk_refs, weight_ref, sems):
    rows = chunk_refs[0].shape[1]
    pairs = [
        (chunk, weight_ref.at[:, rows_at(ranks_ref[0, k], rows), :])
        for k, chunk in enumerate(chunk_refs)
    ]
    return start_copies(pairs, sems)


def expert_forward_kernel(steps, tile, ranks_ref, slots_ref, *refs):
    chunk_refs = refs[:steps]
    out_ref, weight_ref, sems = refs[steps:]
    for copy in load_experts(ranks_ref, chunk_refs, weight_ref, sems):
        copy.wait()
    slots = slots_ref[...]
    total = jnp.zeros(out_ref.shape, F32)
    for at in range(0, weight_ref.shape[2], tile):
        hidden = nn(slots, weight_ref[0, :, at : at + tile])
        active = (hidden * jax.nn.sigmoid(hidden)).astype(BF)
        total = total + nt(active, weight_ref[1, :, at : at + tile])
    out_ref[...] = total.astype(BF)


def expert_backward_kernel(steps, tile, ranks_ref, slots_ref, grad_ref, *refs):
    chunk_refs = refs[:steps]
    back_ref, active_ref, hidden_ref, weight_ref, sems = refs[steps:]
    for copy in load_experts(ranks_ref, chunk_refs, weight_ref, sems):
        copy.wait()
    slots = slots_ref[...]
    grad = grad_ref[...]
    total = jnp.zeros(back_ref.shape, F32)
    for at in range(0, weight_ref.shape[2], tile):
        here = slice(at, at + tile)
        hidden = nn(slots, weight_ref[0, :, here])
        gate = jax.nn.sigmoid(hidden)
        active_ref[:, here] = (hidden * gate).astype(BF)
        hidden_grad = (nn(grad, weight_ref[1, :, here]) * gate * (1.0 + hidden * (1.0 - gate))).astype(BF)
        hidden_ref[:, here] = hidden_grad
        total = total + nt(hidden_grad, weight_ref[0, :, here])
    back_ref[...] = total.astype(BF)


def expert_grads_kernel(steps, tile, ranks_ref, slots_ref, grad_ref, active_ref, hidden_ref, *refs):
    out_refs = refs[:steps]
    sum_ref, sems = refs[steps:]
    slots = slots_ref[...]
    grad = grad_ref[...]
    for at in range(0, active_ref.shape[1], tile):
        here = slice(at, at + tile)
        sum_ref[0, :, here] = tn(slots, hidden_ref[:, here]).astype(BF)
        sum_ref[1, :, here] = tn(grad, active_ref[:, here]).astype(BF)
    rows = out_refs[0].shape[1]
    pairs = [
        (sum_ref.at[:, rows_at(ranks_ref[0, (k + 1) % steps], rows), :], out)
        for k, out in enumerate(out_refs)
    ]
    for copy in start_copies(pairs, sems):
        copy.wait()


def head_lanes(pair_at, shape):
    lane = lax.broadcasted_iota(jnp.int32, shape, 1)
    return (lane < LANES // 2) if pair_at == 0 else (lane >= LANES // 2)


def conv_taps(padded_ref, masks, taps, flip):
    rows = masks.shape[0]
    count = len(taps)
    half = count // 2
    total = jnp.zeros((rows, padded_ref.shape[1]), F32)
    for j in range(count):
        shifted = padded_ref[TAP_PAD + j - half : TAP_PAD + j - half + rows, :]
        tap = taps[count - 1 - j] if flip else taps[j]
        total = total + shifted * masks[:, j : j + 1] * tap
    return total


def middle_forward_kernel(
    dims,
    ranks_ref,
    lengths_ref,
    x0_ref,
    prob_ref,
    cols_ref,
    across_ref,
    returned_ref,
    place_ref,
    extra_ref,
    lines_ref,
    mine_ref,
    other_ref,
    h1_ref,
    h2_ref,
    h3_ref,
    log_ref,
    prob_two_ref,
    slots_ref,
    weight_ref,
    packed_ref,
    blended_ref,
    padded_ref,
    sems,
):
    experts, steps, shard, tap_at, taps_count, gain_at = dims
    core = ranks_ref[2, 0]
    copies = start_copies(
        shared_pairs(mine_ref, other_ref, weight_ref, ranks_ref, core, steps, shard), sems
    )
    rows, width = x0_ref.shape
    bounds = bounds_of(lengths_ref)
    gain = lambda i: lines_ref[gain_at + i : gain_at + i + 1, :]
    prob = prob_ref[...]
    gate = jnp.sum(
        jnp.where(chosen_lanes(cols_ref[:, 0:1], 0, prob.shape), prob, 0.0), axis=-1, keepdims=True
    )
    h1 = x0_ref[...] + 0.5 * (gate * nn(across_ref[...], returned_ref[...]))
    h1_ref[...] = h1
    unit, _ = norm_parts(h1)
    low = (unit * gain(1)).astype(BF)
    for copy in copies:
        copy.wait()
    packed_ref[...] = nn(low, weight_ref[:, : 3 * width]).astype(BF)
    same = segment_of(lax.broadcasted_iota(jnp.int32, (rows, 1), 0), bounds) == segment_of(
        lax.broadcasted_iota(jnp.int32, (1, rows), 1), bounds
    )
    scale = (width // HEADS) ** (-0.5)
    log_lane = lax.broadcasted_iota(jnp.int32, (rows, LANES), 1)
    logs = jnp.zeros((rows, LANES), F32)
    for pair in range(HEADS // 2):
        at = pair * LANES
        query = packed_ref[:, at : at + LANES]
        keys = packed_ref[:, width + at : width + at + LANES]
        values = packed_ref[:, 2 * width + at : 2 * width + at + LANES]
        mixed = None
        for half in range(2):
            mine = head_lanes(half, query.shape)
            scores = nt(jnp.where(mine, query, jnp.zeros_like(query)), keys) * scale
            scores = jnp.where(same, scores, MASKED)
            top = jnp.max(scores, axis=-1, keepdims=True)
            exponent = jnp.exp(scores - top)
            sums = jnp.sum(exponent, axis=-1, keepdims=True)
            weights = (exponent * (1.0 / sums)).astype(BF)
            part = nn(weights, values)
            mixed = part if half == 0 else jnp.where(mine, part, mixed)
            logs = jnp.where(log_lane == 2 * pair + half, top + jnp.log(sums), logs)
        blended_ref[:, at : at + LANES] = mixed.astype(BF)
    log_ref[...] = logs
    h2 = h1 + nn(blended_ref[...], weight_ref[:, 3 * width : 4 * width])
    h2_ref[...] = h2
    unit, _ = norm_parts(h2)
    low = (unit * gain(2)).astype(BF)
    first = nn(low, weight_ref[:, 4 * width : 5 * width])
    second = nn(low, weight_ref[:, 5 * width : 6 * width])
    padded_ref[:TAP_PAD, :] = jnp.zeros((TAP_PAD, width), F32)
    padded_ref[TAP_PAD + rows :, :] = jnp.zeros((TAP_PAD, width), F32)
    padded_ref[TAP_PAD : TAP_PAD + rows, :] = first * jax.nn.sigmoid(second)
    taps = [lines_ref[tap_at + j : tap_at + j + 1, :] for j in range(taps_count)]
    mixed = conv_taps(padded_ref, tap_masks(rows, taps_count // 2, bounds), taps, False)
    active = (mixed * jax.nn.sigmoid(mixed)).astype(BF)
    h3 = h2 + nn(active, weight_ref[:, 6 * width :])
    h3_ref[...] = h3
    unit, _ = norm_parts(h3)
    low = (unit * gain(3)).astype(BF)
    prob_two_ref[...] = lane_softmax(nn(low, extra_ref[...]), experts, experts)
    slots_ref[...] = nn(place_ref[...], low).astype(BF)


def gate_backward(grad, prob, chosen, gate, rows_chosen):
    gate_grad = jnp.sum(grad * rows_chosen, axis=-1, keepdims=True)
    logit_grad = prob * (jnp.where(chosen, gate_grad, 0.0) - gate * gate_grad)
    return logit_grad.astype(BF)


def head_kernel(
    dims,
    ranks_ref,
    lengths_ref,
    frames_ref,
    h3_ref,
    prob_ref,
    cols_ref,
    across_ref,
    returned_ref,
    place_ref,
    lines_ref,
    mine_ref,
    other_ref,
    two_grad_ref,
    logit_grad_ref,
    slots_ref,
    gain_grad_ref,
    loss_ref,
    grad_mine_ref,
    grad_other_ref,
    weight_ref,
    logits_ref,
    grad_ref,
    sems,
):
    experts, steps, shard, gain_at, tile = dims
    core = ranks_ref[2, 0]
    copies = start_copies(
        shared_pairs(mine_ref, other_ref, weight_ref, ranks_ref, core, steps, shard), sems
    )
    rows, width = h3_ref.shape
    vocab = weight_ref.shape[1]
    gain = lines_ref[gain_at + 4 : gain_at + 5, :]
    prob = prob_ref[...]
    chosen = chosen_lanes(cols_ref[:, 1:2], experts, prob.shape)
    gate = jnp.sum(jnp.where(chosen, prob, 0.0), axis=-1, keepdims=True)
    rows_chosen = nn(across_ref[...], returned_ref[...])
    h4 = h3_ref[...] + 0.5 * (gate * rows_chosen)
    unit, scale = norm_parts(h4)
    low = (unit * gain).astype(BF)
    for copy in copies:
        copy.wait()

    def first_pass(i, carry):
        top, sums = carry
        at = pl.multiple_of(i * tile, tile)
        logits = nn(low, weight_ref[:, pl.ds(at, tile)])
        logits_ref[:, pl.ds(at, tile)] = logits
        higher = jnp.maximum(top, jnp.max(logits, axis=-1, keepdims=True))
        sums = sums * jnp.exp(top - higher) + jnp.sum(jnp.exp(logits - higher), axis=-1, keepdims=True)
        return higher, sums

    top, sums = lax.fori_loop(
        0,
        vocab // tile,
        first_pass,
        (jnp.full((rows, 1), -jnp.inf, F32), jnp.zeros((rows, 1), F32)),
    )
    log_total = top + jnp.log(sums)
    _, _, counted_end = bounds_of(lengths_ref)
    counted = (lax.broadcasted_iota(jnp.int32, (rows, 1), 0) < counted_end).astype(F32)
    portion = counted / frames_ref[0, 0]
    target = cols_ref[:, 2:3].astype(jnp.int32)

    def second_pass(i, carry):
        total, picked = carry
        at = pl.multiple_of(i * tile, tile)
        logits = logits_ref[:, pl.ds(at, tile)]
        hit = lax.broadcasted_iota(jnp.int32, (rows, tile), 1) == (target - at)
        picked = picked + jnp.sum(jnp.where(hit, logits, 0.0), axis=-1, keepdims=True)
        guess = jnp.exp(logits - log_total)
        low_grad = (jnp.where(hit, guess - 1.0, guess) * portion).astype(BF)
        grad_ref[:, pl.ds(at, tile)] = tn(low, low_grad).astype(BF)
        return total + nt(low_grad, weight_ref[:, pl.ds(at, tile)]), picked

    total, picked = lax.fori_loop(
        0,
        vocab // tile,
        second_pass,
        (jnp.zeros((rows, width), F32), jnp.zeros((rows, 1), F32)),
    )
    out_copies = start_copies(
        shared_out_pairs(grad_ref, grad_mine_ref, grad_other_ref, ranks_ref, core, steps, shard), sems
    )
    loss = jnp.sum((log_total - picked) * counted, axis=0, keepdims=True)
    loss_ref[...] = jnp.broadcast_to(loss, loss_ref.shape)
    two_grad, gain_grad = norm_back(total, unit, scale, gain)
    two_grad_ref[...] = two_grad
    gain_grad_ref[...] = jnp.broadcast_to(gain_grad, gain_grad_ref.shape)
    half_grad = 0.5 * two_grad
    logit_grad_ref[...] = gate_backward(half_grad, prob, chosen, gate, rows_chosen)
    slots_ref[...] = nn(place_ref[...], (gate * half_grad).astype(BF)).astype(BF)
    for copy in out_copies:
        copy.wait()


def middle_backward_kernel(
    dims,
    ranks_ref,
    lengths_ref,
    two_grad_ref,
    returned_two_ref,
    across_two_ref,
    logit_two_ref,
    h1_ref,
    h2_ref,
    h3_ref,
    log_ref,
    prob_ref,
    cols_ref,
    across_ref,
    returned_ref,
    place_ref,
    extra_ref,
    lines_ref,
    mine_ref,
    other_ref,
    one_grad_ref,
    logit_ref,
    slots_ref,
    small_ref,
    router_ref,
    grad_mine_ref,
    grad_other_ref,
    weight_ref,
    packed_ref,
    packed_grad_ref,
    blended_ref,
    padded_ref,
    padded_grad_ref,
    grad_ref,
    sems,
):
    experts, steps, shard, tap_at, taps_count, gain_at = dims
    core = ranks_ref[2, 0]
    copies = start_copies(
        shared_pairs(mine_ref, other_ref, weight_ref, ranks_ref, core, steps, shard), sems
    )
    rows, width = h1_ref.shape
    bounds = bounds_of(lengths_ref)
    gain = lambda i: lines_ref[gain_at + i : gain_at + i + 1, :]
    small_ref[...] = jnp.zeros(small_ref.shape, F32)
    unit, scale = norm_parts(h3_ref[...])
    low = (unit * gain(3)).astype(BF)
    logit_two = logit_two_ref[...]
    router_ref[...] = tn(logit_two, low)
    back = nn(across_two_ref[...], returned_two_ref[...]) + nt(logit_two, extra_ref[...])
    change, gain_grad = norm_back(back, unit, scale, gain(3))
    small_ref[taps_count : taps_count + 1, :] = gain_grad
    upstream = two_grad_ref[...] + change
    for copy in copies:
        copy.wait()
    upstream_low = upstream.astype(BF)
    unit, scale = norm_parts(h2_ref[...])
    low = (unit * gain(2)).astype(BF)
    first = nn(low, weight_ref[:, 4 * width : 5 * width])
    gate_half = jax.nn.sigmoid(nn(low, weight_ref[:, 5 * width : 6 * width]))
    padded_ref[:TAP_PAD, :] = jnp.zeros((TAP_PAD, width), F32)
    padded_ref[TAP_PAD + rows :, :] = jnp.zeros((TAP_PAD, width), F32)
    padded_ref[TAP_PAD : TAP_PAD + rows, :] = first * gate_half
    taps = [lines_ref[tap_at + j : tap_at + j + 1, :] for j in range(taps_count)]
    masks = tap_masks(rows, taps_count // 2, bounds)
    mixed = conv_taps(padded_ref, masks, taps, False)
    gate_mixed = jax.nn.sigmoid(mixed)
    active = (mixed * gate_mixed).astype(BF)
    grad_ref[:, 6 * width :] = tn(active, upstream_low).astype(BF)
    mixed_grad = (
        nt(upstream_low, weight_ref[:, 6 * width :]) * gate_mixed * (1.0 + mixed * (1.0 - gate_mixed))
    )
    padded_grad_ref[:TAP_PAD, :] = jnp.zeros((TAP_PAD, width), F32)
    padded_grad_ref[TAP_PAD + rows :, :] = jnp.zeros((TAP_PAD, width), F32)
    padded_grad_ref[TAP_PAD : TAP_PAD + rows, :] = mixed_grad
    half = taps_count // 2
    for j in range(taps_count):
        shifted = padded_ref[TAP_PAD + j - half : TAP_PAD + j - half + rows, :]
        small_ref[j : j + 1, :] = jnp.sum(
            shifted * masks[:, j : j + 1] * mixed_grad, axis=0, keepdims=True
        )
    gated_grad = conv_taps(padded_grad_ref, masks, taps, True)
    first_low = (gated_grad * gate_half).astype(BF)
    second_low = (gated_grad * first * gate_half * (1.0 - gate_half)).astype(BF)
    grad_ref[:, 4 * width : 5 * width] = tn(low, first_low).astype(BF)
    grad_ref[:, 5 * width : 6 * width] = tn(low, second_low).astype(BF)
    back = nt(first_low, weight_ref[:, 4 * width : 5 * width]) + nt(
        second_low, weight_ref[:, 5 * width : 6 * width]
    )
    change, gain_grad = norm_back(back, unit, scale, gain(2))
    small_ref[taps_count + 1 : taps_count + 2, :] = gain_grad
    upstream = upstream + change
    upstream_low = upstream.astype(BF)
    unit, scale_norm = norm_parts(h1_ref[...])
    low = (unit * gain(1)).astype(BF)
    packed_ref[...] = nn(low, weight_ref[:, : 3 * width]).astype(BF)
    mixed_low = nt(upstream_low, weight_ref[:, 3 * width : 4 * width]).astype(BF)
    same = segment_of(lax.broadcasted_iota(jnp.int32, (rows, 1), 0), bounds) == segment_of(
        lax.broadcasted_iota(jnp.int32, (1, rows), 1), bounds
    )
    scale = (width // HEADS) ** (-0.5)
    for pair in range(HEADS // 2):
        at = pair * LANES
        query = packed_ref[:, at : at + LANES]
        keys = packed_ref[:, width + at : width + at + LANES]
        values = packed_ref[:, 2 * width + at : 2 * width + at + LANES]
        spread = mixed_low[:, at : at + LANES]
        held = None
        for part in range(2):
            mine = head_lanes(part, query.shape)
            head = 2 * pair + part
            scores = nt(jnp.where(mine, query, jnp.zeros_like(query)), keys) * scale
            scores = jnp.where(same, scores, MASKED)
            probs = jnp.exp(scores - log_ref[:, head : head + 1])
            weights = probs.astype(BF)
            prob_grad = nt(jnp.where(mine, spread, jnp.zeros_like(spread)), values)
            centre = jnp.sum(probs * prob_grad, axis=-1, keepdims=True)
            score_grad = (probs * (prob_grad - centre)).astype(BF)
            found = (
                nn(weights, values),
                tn(weights, spread),
                nn(score_grad, keys) * scale,
                tn(score_grad, query) * scale,
            )
            held = found if part == 0 else tuple(jnp.where(mine, new, old) for new, old in zip(found, held))
        blended_ref[:, at : at + LANES] = held[0].astype(BF)
        packed_grad_ref[:, 2 * width + at : 2 * width + at + LANES] = held[1].astype(BF)
        packed_grad_ref[:, at : at + LANES] = held[2].astype(BF)
        packed_grad_ref[:, width + at : width + at + LANES] = held[3].astype(BF)
    grad_ref[:, 3 * width : 4 * width] = tn(blended_ref[...], upstream_low).astype(BF)
    packed_grad = packed_grad_ref[...]
    grad_ref[:, : 3 * width] = tn(low, packed_grad).astype(BF)
    out_copies = start_copies(
        shared_out_pairs(grad_ref, grad_mine_ref, grad_other_ref, ranks_ref, core, steps, shard), sems
    )
    change, gain_grad = norm_back(
        nt(packed_grad, weight_ref[:, : 3 * width]), unit, scale_norm, gain(1)
    )
    small_ref[taps_count + 2 : taps_count + 3, :] = gain_grad
    one_grad = upstream + change
    one_grad_ref[...] = one_grad
    prob = prob_ref[...]
    chosen = chosen_lanes(cols_ref[:, 0:1], 0, prob.shape)
    gate = jnp.sum(jnp.where(chosen, prob, 0.0), axis=-1, keepdims=True)
    half_grad = 0.5 * one_grad
    rows_chosen = nn(across_ref[...], returned_ref[...])
    logit_ref[...] = gate_backward(half_grad, prob, chosen, gate, rows_chosen)
    slots_ref[...] = nn(place_ref[...], (gate * half_grad).astype(BF)).astype(BF)
    for copy in out_copies:
        copy.wait()


def back_kernel(
    dims,
    one_grad_ref,
    returned_ref,
    across_ref,
    logit_ref,
    x0_ref,
    feat_ref,
    extra_ref,
    lines_ref,
    small_ref,
    router_ref,
    gain_four_ref,
    out_ref,
    lines_grad_ref,
):
    experts, tap_at, taps_count, gain_at = dims
    feats = feat_ref.shape[0]
    unit, scale = norm_parts(x0_ref[...])
    gain = lines_ref[gain_at : gain_at + 1, :]
    low = (unit * gain).astype(BF)
    logit = logit_ref[...]
    back = nn(across_ref[...], returned_ref[...]) + nt(logit, extra_ref[...])
    change, gain_grad = norm_back(back, unit, scale, gain)
    embedded_low = (one_grad_ref[...] + change).astype(BF)
    lines_grad_ref[...] = tn(logit, low) + router_ref[...]
    lines_grad_ref[2 * experts : 2 * experts + feats, :] = nn(feat_ref[...], embedded_low)
    lines_grad_ref[tap_at : tap_at + taps_count, :] = small_ref[:taps_count, :]
    lines_grad_ref[gain_at : gain_at + 1, :] = gain_grad
    lines_grad_ref[gain_at + 1 : gain_at + 2, :] = small_ref[taps_count + 2 : taps_count + 3, :]
    lines_grad_ref[gain_at + 2 : gain_at + 3, :] = small_ref[taps_count + 1 : taps_count + 2, :]
    lines_grad_ref[gain_at + 3 : gain_at + 4, :] = small_ref[taps_count : taps_count + 1, :]
    lines_grad_ref[gain_at + 4 : gain_at + 5, :] = gain_four_ref[0:1, :]
    out_ref[...] = lines_grad_ref[...].T.astype(BF)


def spec(kind):
    space = {"v": pltpu.VMEM, "s": pltpu.SMEM, "a": pl.ANY}[kind]
    return pl.BlockSpec(memory_space=space)


def shaped(shape, dtype):
    return jax.ShapeDtypeStruct(shape, dtype)


def call(kernel, name, kinds, args, outs, out_kinds, scratch=(), flops=0, moved=0):
    return pl.pallas_call(
        kernel,
        name=name,
        out_shape=tuple(outs),
        in_specs=[spec(kind) for kind in kinds],
        out_specs=tuple(spec(kind) for kind in out_kinds),
        scratch_shapes=list(scratch),
        compiler_params=pltpu.CompilerParams(vmem_limit_bytes=VMEM_BYTES),
        cost_estimate=pl.CostEstimate(flops=int(flops), bytes_accessed=int(moved), transcendentals=0),
    )(*args)


def ring_order(size):
    return list(range(0, size, 2)) + list(range(size - 1 - (size % 2), 0, -2))


def ring_pairs(size, experts):
    order = ring_order(size)
    pairs = []
    for place in range(size):
        for e in range(experts):
            step = 1 if e % 2 == 0 else -1
            pairs.append((order[place] * experts + e, order[(place + step) % size] * experts + e))
    return pairs


def rank_table(size):
    order = ring_order(size)
    where = {rank: place for place, rank in enumerate(order)}
    table = np.zeros((size, 2, size), np.int32)
    for rank in range(size):
        for core in range(2):
            step = 1 if core == 0 else -1
            for k in range(size):
                table[rank, core, k] = order[(where[rank] - step * k) % size]
    return table


def ring_step(array, pairs):
    return lax.ppermute(array, ALL, pairs)


def ring_gather(shard, pairs, size):
    chunks = [shard]
    for _ in range(size - 1):
        chunks.append(ring_step(chunks[-1], pairs))
    return chunks


def core_swap(array, experts):
    return lax.ppermute(array, "expert", [(e, e ^ 1) for e in range(experts)])


def over_chips(array, experts):
    total = array.astype(F32)
    chips = experts // 2
    for shift in range(1, chips):
        moved = lax.ppermute(
            array, "expert", [(e, (e // 2 + shift) % chips * 2 + e % 2) for e in range(experts)]
        )
        total = total + moved.astype(F32)
    return total


def swap_rows(slots, experts):
    parts = slots.reshape(experts, slots.shape[0] // experts, slots.shape[1])
    return lax.all_to_all(parts, "expert", split_axis=0, concat_axis=0, tiled=True).reshape(slots.shape)


def shared_scatter(mine, other, pairs, size, experts, core):
    arrived = core_swap(other, experts)
    partial = (mine[0] + arrived[0]).astype(BF)
    for k in range(1, size):
        partial = ring_step(partial, pairs) + (mine[k] + arrived[k])
    own = over_chips(partial, experts).astype(BF)
    far = core_swap(own, experts)
    return jnp.where(core == 0, jnp.concatenate([own, far], 1), jnp.concatenate([far, own], 1))


def expert_scatter(chunks, pairs):
    partial = chunks[0]
    for chunk in chunks[1:]:
        partial = ring_step(partial, pairs) + chunk
    return partial


def adamw(gradient, master, moment, square, rate, decay):
    moment = BETA_ONE * moment + (1.0 - BETA_ONE) * gradient
    square = BETA_TWO * square + (1.0 - BETA_TWO) * gradient * gradient
    update = (
        moment / (1.0 - BETA_ONE**STEP) / (jnp.sqrt(square / (1.0 - BETA_TWO**STEP)) + ADAM_EPS)
    )
    return (moment, square, master - rate * (update + decay * master))


def on_device(features, lengths, routes, alignment, *weights):
    copies, masters, firsts, seconds = (weights[8 * i : 8 * i + 8] for i in range(4))
    attend_copy, output_copy, conv_copy, head_copy, extra_copy, gains_copy, up_copy, down_copy = copies
    size = lax.axis_size("dp")
    experts = lax.axis_size("expert")
    dp_at = lax.axis_index("dp")
    expert_at = lax.axis_index("expert")
    core = expert_at % 2
    row_count, feat_count = features.shape
    shard = attend_copy.shape[0]
    width = shard * size
    vocab = head_copy.shape[1]
    units = up_copy.shape[3]
    aux = extra_copy.shape[1]
    taps_count = aux - 2 * experts - feat_count
    tap_at = 2 * experts + feat_count
    gain_at = aux
    capacity = row_count * 5 // (4 * experts)
    slot_count = experts * capacity
    pairs = ring_pairs(size, experts)
    table = jnp.asarray(rank_table(size))[dp_at]
    ranks = jnp.concatenate(
        [
            lax.dynamic_index_in_dim(table, core, 0, keepdims=True),
            lax.dynamic_index_in_dim(table, 1 - core, 0, keepdims=True),
            jnp.full((1, size), core, jnp.int32),
        ]
    )

    pack = jnp.concatenate(
        [extra_copy, gains_copy.T, jnp.zeros((shard, LANES - aux - gains_copy.shape[0]), BF)], axis=1
    )
    extra = lax.all_to_all(
        jnp.broadcast_to(pack[None], (size,) + pack.shape), "dp", split_axis=0, concat_axis=0, tiled=True
    ).reshape(width, LANES)
    everyone = size * experts
    frames_here = (row_count - lengths[0, 3]).astype(F32)
    frame_count = jnp.sum(
        lax.all_to_all(
            jnp.broadcast_to(frames_here, (everyone, 1, LANES)), ALL, split_axis=0, concat_axis=0, tiled=True
        )[:, 0, 0]
    )

    expert_shards = [
        jnp.stack([up_copy[f, 0], down_copy[f, 0].T]) for f in range(2)
    ]
    first_chunks = ring_gather(expert_shards[0], pairs, size)
    second_chunks = ring_gather(expert_shards[1], pairs, size)
    shared = jnp.concatenate([attend_copy, output_copy, conv_copy], axis=1)
    half_shared = shared.shape[1] // 2
    shared_mine = jnp.stack(
        ring_gather(lax.dynamic_slice_in_dim(shared, core * half_shared, half_shared, 1), pairs, size)
    )
    shared_other = core_swap(shared_mine, experts)
    half_vocab = vocab // 2
    head_mine = jnp.stack(
        ring_gather(lax.dynamic_slice_in_dim(head_copy, core * half_vocab, half_vocab, 1), pairs, size)
    )
    head_other = core_swap(head_mine, experts)

    square = (row_count, width)
    lanes = (row_count, LANES)
    cols, place_one, across_one, place_two, across_two = call(
        functools.partial(routing_kernel, capacity),
        "routing",
        "vv",
        (jnp.swapaxes(routes, 1, 2), alignment[None, :]),
        [shaped(lanes, F32)]
        + [shaped((slot_count, row_count), BF), shaped((row_count, slot_count), BF)] * 2,
        "vvvvv",
    )
    features_across = features.T

    def front(feat_ref, extra_ref, place_ref, *outs):
        front_kernel(experts, feat_ref, extra_ref, place_ref, gain_at, *outs)

    x0, slots_one, prob_one, lines = call(
        front,
        "front",
        "vvv",
        (features_across, extra, place_one),
        [shaped(square, F32), shaped((slot_count, width), BF), shaped(lanes, F32), shaped((LANES, width), F32)],
        "vvvv",
        flops=1e9,
        moved=4e6,
    )
    expert_scratch = [pltpu.VMEM((2, width, units), BF), pltpu.SemaphoreType.DMA((size,))]
    tile = 512

    def expert_forward(slots, chunks):
        return call(
            functools.partial(expert_forward_kernel, size, tile),
            "expert_forward",
            "sv" + "a" * size,
            (ranks, slots, *chunks),
            [shaped(slots.shape, BF)],
            "v",
            expert_scratch,
            flops=4.0 * slot_count * width * units,
            moved=6e6,
        )[0]

    received_one = swap_rows(slots_one, experts)
    returned_one = swap_rows(expert_forward(received_one, first_chunks), experts)
    copy_sems = pltpu.SemaphoreType.DMA((2 * size,))
    middle_dims = (experts, size, shard, tap_at, taps_count, gain_at)
    h1, h2, h3, logs, prob_two, slots_two = call(
        functools.partial(middle_forward_kernel, middle_dims),
        "middle_forward",
        "ssvvvvvvvvaa",
        (
            ranks,
            lengths,
            x0,
            prob_one,
            cols,
            across_one,
            returned_one,
            place_two,
            extra,
            lines,
            shared_mine,
            shared_other,
        ),
        [shaped(square, F32)] * 3
        + [shaped(lanes, F32), shaped(lanes, F32), shaped((slot_count, width), BF)],
        "vvvvvv",
        [
            pltpu.VMEM((width, 7 * width), BF),
            pltpu.VMEM((row_count, 3 * width), BF),
            pltpu.VMEM(square, BF),
            pltpu.VMEM((row_count + 2 * TAP_PAD, width), F32),
            copy_sems,
        ],
        flops=12e9,
        moved=10e6,
    )
    received_two = swap_rows(slots_two, experts)
    returned_two = swap_rows(expert_forward(received_two, second_chunks), experts)
    two_grad, logit_two, grad_slots_two, gain_four, loss_part, head_grad_mine, head_grad_other = call(
        functools.partial(head_kernel, (experts, size, shard, gain_at, 1024)),
        "head",
        "sssvvvvvvvaa",
        (
            ranks,
            lengths,
            frame_count.reshape(1, 1),
            h3,
            prob_two,
            cols,
            across_two,
            returned_two,
            place_two,
            lines,
            head_mine,
            head_other,
        ),
        [
            shaped(square, F32),
            shaped(lanes, BF),
            shaped((slot_count, width), BF),
            shaped((8, width), F32),
            shaped((8, LANES), F32),
            shaped((size, shard, half_vocab), BF),
            shaped((size, shard, half_vocab), BF),
        ],
        "vvvvvaa",
        [
            pltpu.VMEM((width, vocab), BF),
            pltpu.VMEM((row_count, vocab), F32),
            pltpu.VMEM((width, vocab), BF),
            copy_sems,
        ],
        flops=20e9,
        moved=20e6,
    )

    def expert_backward(slots, grads, chunks):
        back, active, hidden = call(
            functools.partial(expert_backward_kernel, size, tile),
            "expert_backward",
            "svv" + "a" * size,
            (ranks, slots, grads, *chunks),
            [shaped(slots.shape, BF), shaped((slot_count, units), BF), shaped((slot_count, units), BF)],
            "vvv",
            expert_scratch,
            flops=6.0 * slot_count * width * units,
            moved=12e6,
        )
        sums = call(
            functools.partial(expert_grads_kernel, size, tile),
            "expert_grads",
            "svvvv",
            (ranks, slots, grads, active, hidden),
            [shaped((2, shard, units), BF)] * size,
            "a" * size,
            expert_scratch,
            flops=4.0 * slot_count * width * units,
            moved=10e6,
        )
        return back, sums

    out_grad_two = swap_rows(grad_slots_two, experts)
    back_two, sums_two = expert_backward(received_two, out_grad_two, second_chunks)
    slot_grad_two = swap_rows(back_two, experts)
    one_grad, logit_one, grad_slots_one, small, router_two, mid_grad_mine, mid_grad_other = call(
        functools.partial(middle_backward_kernel, middle_dims),
        "middle_backward",
        "ss" + "v" * 15 + "aa",
        (
            ranks,
            lengths,
            two_grad,
            slot_grad_two,
            across_two,
            logit_two,
            h1,
            h2,
            h3,
            logs,
            prob_one,
            cols,
            across_one,
            returned_one,
            place_one,
            extra,
            lines,
            shared_mine,
            shared_other,
        ),
        [
            shaped(square, F32),
            shaped(lanes, BF),
            shaped((slot_count, width), BF),
            shaped((24, width), F32),
            shaped((LANES, width), F32),
            shaped((size, shard, half_shared), BF),
            shaped((size, shard, half_shared), BF),
        ],
        "vvvvvaa",
        [
            pltpu.VMEM((width, 7 * width), BF),
            pltpu.VMEM((row_count, 3 * width), BF),
            pltpu.VMEM((row_count, 3 * width), BF),
            pltpu.VMEM(square, BF),
            pltpu.VMEM((row_count + 2 * TAP_PAD, width), F32),
            pltpu.VMEM((row_count + 2 * TAP_PAD, width), F32),
            pltpu.VMEM((width, 7 * width), BF),
            copy_sems,
        ],
        flops=25e9,
        moved=20e6,
    )
    out_grad_one = swap_rows(grad_slots_one, experts)
    back_one, sums_one = expert_backward(received_one, out_grad_one, first_chunks)
    slot_grad_one = swap_rows(back_one, experts)
    (extra_grad,) = call(
        functools.partial(back_kernel, (experts, tap_at, taps_count, gain_at)),
        "back",
        "v" * 11,
        (
            one_grad,
            slot_grad_one,
            across_one,
            logit_one,
            x0,
            features_across,
            extra,
            lines,
            small,
            router_two,
            gain_four,
        ),
        [shaped((width, LANES), BF)],
        "v",
        [pltpu.VMEM((LANES, width), F32)],
        flops=2e9,
        moved=5e6,
    )

    head_sum = shared_scatter(head_grad_mine, head_grad_other, pairs, size, experts, core).astype(F32)
    sums_two = expert_scatter(sums_two, pairs)
    mid_sum = shared_scatter(mid_grad_mine, mid_grad_other, pairs, size, experts, core).astype(F32)
    sums_one = expert_scatter(sums_one, pairs)
    spread = jnp.broadcast_to(
        extra_grad.reshape(size, 1, shard, LANES), (size, experts, shard, LANES)
    ).reshape(everyone, shard, LANES)
    small_sum = jnp.sum(
        lax.all_to_all(spread, ALL, split_axis=0, concat_axis=0, tiled=True).astype(F32), axis=0
    )
    extra_sum = small_sum[:, :aux]
    gains_sum = small_sum[:, aux : aux + gains_copy.shape[0]].T
    attend_sum = mid_sum[:, : 3 * width]
    output_sum = mid_sum[:, 3 * width : 4 * width]
    conv_sum = mid_sum[:, 4 * width :]
    up_sum = jnp.stack([sums_one[0], sums_two[0]])[:, None].astype(F32)
    down_sum = jnp.stack([sums_one[1], sums_two[1]])[:, None].astype(F32)
    shared_squares = jnp.float32(0.0)
    for member in (mid_sum, head_sum, extra_sum, gains_sum):
        shared_squares = shared_squares + jnp.sum(member * member)
    expert_squares = jnp.sum(up_sum * up_sum) + jnp.sum(down_sum * down_sum)
    local_squares = jnp.where(expert_at == 0, shared_squares, 0.0) + expert_squares
    totals = jnp.stack([local_squares, loss_part[0, 0]])
    totals = jnp.sum(
        lax.all_to_all(
            jnp.broadcast_to(totals[None, :, None], (everyone, 2, LANES)),
            ALL,
            split_axis=0,
            concat_axis=0,
            tiled=True,
        )[:, :, 0],
        axis=0,
    )
    global_norm = jnp.sqrt(totals[0])
    loss_sum = totals[1]
    factor = jnp.minimum(1.0, 0.1 * math.sqrt(width / (row_count * everyone)) / global_norm)
    gradients = (attend_sum, output_sum, conv_sum, head_sum, extra_sum, gains_sum, up_sum, down_sum)
    turned = lambda arrays: arrays[:7] + (jnp.swapaxes(arrays[7], 2, 3),)
    results = [
        adamw(gradient * factor, master, moment, second, rate, decay)
        for gradient, master, moment, second, rate, decay in zip(
            gradients, turned(masters), turned(firsts), turned(seconds), STEP_RATES, DECAYS
        )
    ]
    results[7] = tuple(jnp.swapaxes(member, 2, 3) for member in results[7])
    return (
        loss_sum,
        frame_count,
        global_norm,
        *(result[0] for result in results),
        *(result[1] for result in results),
        *(result[2] for result in results),
    )


def solution(mesh):
    weight_specs = (
        P("dp", None),
        P("dp", None),
        P("dp", None),
        P("dp", None),
        P("dp", None),
        P(None, "dp"),
        P(None, "expert", "dp", None),
        P(None, "expert", None, "dp"),
    )
    return jax.shard_map(
        on_device,
        mesh=mesh,
        in_specs=(
            P(("dp", "expert"), None),
            P(("dp", "expert"), None),
            P(None, ("dp", "expert"), None),
            P(("dp", "expert")),
        )
        + weight_specs * 4,
        out_specs=(P(), P(), P()) + weight_specs * 3,
        check_vma=False,
    )
```

```python
import functools
import math

import jax
import jax.numpy as jnp
import numpy as np
from jax import lax
from jax.experimental import pallas as pl
from jax.experimental.pallas import tpu as pltpu
from jax.sharding import PartitionSpec as P

HEADS = 8
STEP = 5
NORM_EPS = 1e-05
ADAM_EPS = 1e-08
BETA_ONE = 0.5
BETA_TWO = 0.5
MASKED = -1000000000.0
STEP_RATES = (0.02, 0.2, 0.02, 0.05, 0.05, 0.5, 0.02, 0.1)
DECAYS = (0.01, 0.01, 0.01, 0.01, 0.01, 0.0, 0.01, 0.01)

BF = jnp.bfloat16
F32 = jnp.float32
ALL = ("dp", "expert")
VMEM_BYTES = 56 * 1024 * 1024
LANES = 128
TAP_PAD = 16
TAP_ROWS = 256


def nn(left, right):
    return jnp.dot(left, right, preferred_element_type=F32)


def nt(left, right):
    return lax.dot_general(left, right, (((1,), (1,)), ((), ())), preferred_element_type=F32)


def tn(left, right):
    return lax.dot_general(left, right, (((0,), (0,)), ((), ())), preferred_element_type=F32)


def norm_parts(values):
    centred = values - jnp.mean(values, axis=-1, keepdims=True)
    scale = lax.rsqrt(jnp.mean(centred * centred, axis=-1, keepdims=True) + NORM_EPS)
    return centred * scale, scale


def norm_back(grad, unit, scale, gain_row):
    weighted = grad * gain_row
    mean = jnp.mean(weighted, axis=-1, keepdims=True)
    along = jnp.mean(weighted * unit, axis=-1, keepdims=True)
    gain_grad = jnp.sum(grad * unit, axis=0, keepdims=True)
    return scale * (weighted - mean - unit * along), gain_grad


def lane_softmax(logits, first, count):
    lane = lax.broadcasted_iota(jnp.int32, logits.shape, 1)
    inside = (lane >= first) & (lane < first + count)
    logits = jnp.where(inside, logits, -jnp.inf)
    weight = jnp.exp(logits - jnp.max(logits, axis=-1, keepdims=True))
    return weight / jnp.sum(weight, axis=-1, keepdims=True)


def chosen_lanes(route_col, first, shape):
    lane = lax.broadcasted_iota(jnp.int32, shape, 1)
    return lane == (route_col.astype(jnp.int32) + first)


def bounds_of(lengths_ref):
    first = lengths_ref[0, 0]
    second = first + lengths_ref[0, 1]
    return first, second, second + lengths_ref[0, 2]


def segment_of(places, bounds):
    total = jnp.zeros(places.shape, jnp.int32)
    for bound in bounds:
        total = total + (places >= bound).astype(jnp.int32)
    return total


def tap_masks(rows, half_span, bounds):
    place = lax.broadcasted_iota(jnp.int32, (rows, LANES), 0)
    lane = lax.broadcasted_iota(jnp.int32, (rows, LANES), 1)
    same = segment_of(place, bounds) == segment_of(place + lane - half_span, bounds)
    return same.astype(F32)


def start_copies(pairs, sems):
    copies = [pltpu.make_async_copy(src, dst, sems.at[i]) for i, (src, dst) in enumerate(pairs)]
    for copy in copies:
        copy.start()
    return copies


def rows_at(rank, rows):
    return pl.ds(pl.multiple_of(rank * rows, rows), rows)


def shared_pairs(mine_ref, other_ref, full_ref, ranks_ref, core, steps, rows):
    width = mine_ref.shape[-1]
    own = pl.ds(pl.multiple_of(core * width, LANES), width)
    far = pl.ds(pl.multiple_of((1 - core) * width, LANES), width)
    pairs = []
    for k in range(steps):
        pairs.append((mine_ref.at[k], full_ref.at[rows_at(ranks_ref[0, k], rows), own]))
        pairs.append((other_ref.at[k], full_ref.at[rows_at(ranks_ref[1, k], rows), far]))
    return pairs


def shared_out_pairs(full_ref, mine_ref, other_ref, ranks_ref, core, steps, rows):
    width = mine_ref.shape[-1]
    own = pl.ds(pl.multiple_of(core * width, LANES), width)
    far = pl.ds(pl.multiple_of((1 - core) * width, LANES), width)
    pairs = []
    for k in range(steps):
        later = (k + 1) % steps
        pairs.append((full_ref.at[rows_at(ranks_ref[0, later], rows), own], mine_ref.at[k]))
        pairs.append((full_ref.at[rows_at(ranks_ref[1, later], rows), far], other_ref.at[k]))
    return pairs


def half_pairs(mine_ref, other_ref, full_ref, core):
    width = mine_ref.shape[-1]
    own = pl.ds(pl.multiple_of(core * width, LANES), width)
    partner = pl.ds(pl.multiple_of((1 - core) * width, LANES), width)
    return [(mine_ref, full_ref.at[:, own]), (other_ref, full_ref.at[:, partner])]


def routing_kernel(capacity, routes_ref, align_ref, cols_ref, *place_refs):
    rows = routes_ref.shape[2]
    before = (
        lax.broadcasted_iota(jnp.int32, (rows, rows), 0)
        < lax.broadcasted_iota(jnp.int32, (rows, rows), 1)
    ).astype(BF)
    kept = []
    slots = []
    for f in range(2):
        route_row = routes_ref[f]
        named = lax.broadcasted_iota(jnp.int32, (16, rows), 0) == route_row
        counts = nn(named.astype(BF), before)
        rank = jnp.sum(jnp.where(named, counts, 0.0), axis=0, keepdims=True)
        slots.append(route_row.astype(F32) * capacity + rank)
        kept.append(route_row.astype(F32))
    lines = jnp.concatenate(
        kept + [align_ref[...].astype(F32)] + slots + [jnp.zeros((LANES - 5, rows), F32)], axis=0
    )
    cols = lines.T
    cols_ref[...] = cols
    for f in range(2):
        down_ref, across_ref = place_refs[2 * f], place_refs[2 * f + 1]
        slot_count = down_ref.shape[0]
        slot_row = slots[f].astype(jnp.int32)
        slot_col = cols[:, 3 + f : 4 + f].astype(jnp.int32)
        down_ref[...] = (
            lax.broadcasted_iota(jnp.int32, (slot_count, rows), 0) == slot_row
        ).astype(BF)
        across_ref[...] = (
            lax.broadcasted_iota(jnp.int32, (rows, slot_count), 1) == slot_col
        ).astype(BF)


def front_kernel(experts, feat_ref, extra_ref, place_ref, gain_at, x0_ref, slots_ref, prob_ref, lines_ref):
    extra = extra_ref[...]
    lines_ref[...] = extra.astype(F32).T
    feats = feat_ref.shape[0]
    table = lines_ref[2 * experts : 2 * experts + feats, :].astype(BF)
    embedded = tn(feat_ref[...], table)
    x0_ref[...] = embedded
    unit, _ = norm_parts(embedded)
    low = (unit * lines_ref[gain_at : gain_at + 1, :]).astype(BF)
    prob_ref[...] = lane_softmax(nn(low, extra), 0, experts)
    slots_ref[...] = nn(place_ref[...], low).astype(BF)


def load_experts(tile, ranks_ref, chunk_refs, weight_ref, sems):
    rows = chunk_refs[0].shape[1]
    groups = []
    for i in range(weight_ref.shape[2] // tile):
        columns = pl.ds(i * tile, tile)
        pairs = [
            (chunk.at[:, :, columns], weight_ref.at[:, rows_at(ranks_ref[0, k], rows), columns])
            for k, chunk in enumerate(chunk_refs)
        ]
        groups.append(start_copies(pairs, sems.at[i]))
    return groups


def expert_forward_kernel(steps, tile, ranks_ref, slots_ref, *refs):
    chunk_refs = refs[:steps]
    out_ref, weight_ref, sems = refs[steps:]
    groups = load_experts(tile, ranks_ref, chunk_refs, weight_ref, sems)
    slots = slots_ref[...]
    total = jnp.zeros(out_ref.shape, F32)
    for at in range(0, weight_ref.shape[2], tile):
        for copy in groups[at // tile]:
            copy.wait()
        hidden = nn(slots, weight_ref[0, :, at : at + tile])
        active = (hidden * jax.nn.sigmoid(hidden)).astype(BF)
        total = total + nt(active, weight_ref[1, :, at : at + tile])
    out_ref[...] = total.astype(BF)


def expert_backward_kernel(steps, tile, ranks_ref, slots_ref, grad_ref, *refs):
    chunk_refs = refs[:steps]
    back_ref, active_ref, hidden_ref, weight_ref, sems = refs[steps:]
    groups = load_experts(tile, ranks_ref, chunk_refs, weight_ref, sems)
    slots = slots_ref[...]
    grad = grad_ref[...]
    total = jnp.zeros(back_ref.shape, F32)
    for at in range(0, weight_ref.shape[2], tile):
        here = slice(at, at + tile)
        for copy in groups[at // tile]:
            copy.wait()
        hidden = nn(slots, weight_ref[0, :, here])
        gate = jax.nn.sigmoid(hidden)
        active_ref[:, here] = (hidden * gate).astype(BF)
        hidden_grad = (nn(grad, weight_ref[1, :, here]) * gate * (1.0 + hidden * (1.0 - gate))).astype(BF)
        hidden_ref[:, here] = hidden_grad
        total = total + nt(hidden_grad, weight_ref[0, :, here])
    back_ref[...] = total.astype(BF)


def expert_grads_kernel(steps, tile, ranks_ref, slots_ref, grad_ref, active_ref, hidden_ref, *refs):
    out_refs = refs[:steps]
    sum_ref, sems = refs[steps:]
    slots = slots_ref[...].T
    grad = grad_ref[...].T
    for at in range(0, active_ref.shape[1], tile):
        here = slice(at, at + tile)
        sum_ref[0, :, here] = nn(slots, hidden_ref[:, here]).astype(BF)
        sum_ref[1, :, here] = nn(grad, active_ref[:, here]).astype(BF)
    rows = out_refs[0].shape[1]
    pairs = [
        (sum_ref.at[:, rows_at(ranks_ref[0, (k + 1) % steps], rows), :], out)
        for k, out in enumerate(out_refs)
    ]
    for copy in start_copies(pairs, sems):
        copy.wait()


def head_lanes(pair_at, shape):
    lane = lax.broadcasted_iota(jnp.int32, shape, 1)
    return (lane < LANES // 2) if pair_at == 0 else (lane >= LANES // 2)


def tap_window(padded_ref, base, half_span):
    start = base + TAP_PAD - half_span
    return lambda j: padded_ref[start + j : start + j + TAP_ROWS, :]


def clear_edges(padded_ref):
    edge = jnp.zeros((TAP_PAD, padded_ref.shape[1]), F32)
    padded_ref[:TAP_PAD, :] = edge
    padded_ref[padded_ref.shape[0] - TAP_PAD :, :] = edge


def conv_rows(padded_ref, masks_ref, taps, out_ref):
    count = len(taps)

    for base in range(0, masks_ref.shape[0], TAP_ROWS):
        shifted = tap_window(padded_ref, base, count // 2)
        masks = masks_ref[pl.ds(base, TAP_ROWS), :]
        total = jnp.zeros((TAP_ROWS, padded_ref.shape[1]), F32)
        for j in range(count):
            total = total + shifted(j) * masks[:, j : j + 1] * taps[j]
        out_ref[pl.ds(base, TAP_ROWS), :] = total


def conv_rows_back(padded_ref, padded_grad_ref, masks_ref, taps, out_ref, sums_ref):
    count = len(taps)
    width = padded_ref.shape[1]
    sums_ref[...] = jnp.zeros(sums_ref.shape, F32)

    for base in range(0, masks_ref.shape[0], TAP_ROWS):
        values = tap_window(padded_ref, base, count // 2)
        grads = tap_window(padded_grad_ref, base, count // 2)
        masks = masks_ref[pl.ds(base, TAP_ROWS), :]
        here = grads(count // 2)
        total = jnp.zeros((TAP_ROWS, width), F32)
        for j in range(count):
            mask = masks[:, j : j + 1]
            total = total + grads(j) * mask * taps[count - 1 - j]
            part = values(j) * mask * here
            sums_ref[j] += jnp.sum(part.reshape(TAP_ROWS // 8, 8, width), axis=0)
        out_ref[pl.ds(base, TAP_ROWS), :] = total


def middle_forward_kernel(
    dims,
    ranks_ref,
    lengths_ref,
    x0_ref,
    prob_ref,
    cols_ref,
    across_ref,
    returned_ref,
    place_ref,
    extra_ref,
    lines_ref,
    mine_ref,
    other_ref,
    h1_ref,
    h2_ref,
    h3_ref,
    log_ref,
    prob_two_ref,
    slots_ref,
    mixed_ref,
    packed_ref,
    blended_ref,
    weight_ref,
    padded_ref,
    masks_ref,
    sems,
):
    experts, steps, shard, tap_at, taps_count, gain_at = dims
    core = ranks_ref[2, 0]
    copies = start_copies(
        shared_pairs(mine_ref, other_ref, weight_ref, ranks_ref, core, steps, shard), sems
    )
    rows, width = x0_ref.shape
    bounds = bounds_of(lengths_ref)
    gain = lambda i: lines_ref[gain_at + i : gain_at + i + 1, :]
    prob = prob_ref[...]
    gate = jnp.sum(
        jnp.where(chosen_lanes(cols_ref[:, 0:1], 0, prob.shape), prob, 0.0), axis=-1, keepdims=True
    )
    h1 = x0_ref[...] + 0.5 * (gate * nn(across_ref[...], returned_ref[...]))
    h1_ref[...] = h1
    unit, _ = norm_parts(h1)
    low = (unit * gain(1)).astype(BF)
    for copy in copies:
        copy.wait()
    packed_ref[...] = nn(low, weight_ref[:, : 3 * width]).astype(BF)
    same = segment_of(lax.broadcasted_iota(jnp.int32, (rows, 1), 0), bounds) == segment_of(
        lax.broadcasted_iota(jnp.int32, (1, rows), 1), bounds
    )
    scale = (width // HEADS) ** (-0.5)
    log_lane = lax.broadcasted_iota(jnp.int32, (rows, LANES), 1)
    logs = jnp.zeros((rows, LANES), F32)
    for pair in range(HEADS // 2):
        at = pair * LANES
        query = packed_ref[:, at : at + LANES]
        keys = packed_ref[:, width + at : width + at + LANES]
        values = packed_ref[:, 2 * width + at : 2 * width + at + LANES]
        mixed = None
        for half in range(2):
            mine = head_lanes(half, query.shape)
            scores = nt(jnp.where(mine, query, jnp.zeros_like(query)), keys) * scale
            scores = jnp.where(same, scores, MASKED)
            top = jnp.max(scores, axis=-1, keepdims=True)
            exponent = jnp.exp(scores - top)
            sums = jnp.sum(exponent, axis=-1, keepdims=True)
            weights = (exponent * (1.0 / sums)).astype(BF)
            part = nn(weights, values)
            mixed = part if half == 0 else jnp.where(mine, part, mixed)
            logs = jnp.where(log_lane == 2 * pair + half, top + jnp.log(sums), logs)
        blended_ref[:, at : at + LANES] = mixed.astype(BF)
    log_ref[...] = logs
    h2 = h1 + nn(blended_ref[...], weight_ref[:, 3 * width : 4 * width])
    h2_ref[...] = h2
    unit, _ = norm_parts(h2)
    low = (unit * gain(2)).astype(BF)
    first = nn(low, weight_ref[:, 4 * width : 5 * width])
    second = nn(low, weight_ref[:, 5 * width : 6 * width])
    clear_edges(padded_ref)
    padded_ref[TAP_PAD : TAP_PAD + rows, :] = first * jax.nn.sigmoid(second)
    masks_ref[...] = tap_masks(rows, taps_count // 2, bounds)
    taps = [lines_ref[tap_at + j : tap_at + j + 1, :] for j in range(taps_count)]
    conv_rows(padded_ref, masks_ref, taps, mixed_ref)
    mixed = mixed_ref[...]
    active = (mixed * jax.nn.sigmoid(mixed)).astype(BF)
    h3 = h2 + nn(active, weight_ref[:, 6 * width :])
    h3_ref[...] = h3
    unit, _ = norm_parts(h3)
    low = (unit * gain(3)).astype(BF)
    prob_two_ref[...] = lane_softmax(nn(low, extra_ref[...]), experts, experts)
    slots_ref[...] = nn(place_ref[...], low).astype(BF)


def gate_backward(grad, prob, chosen, gate, rows_chosen):
    gate_grad = jnp.sum(grad * rows_chosen, axis=-1, keepdims=True)
    logit_grad = prob * (jnp.where(chosen, gate_grad, 0.0) - gate * gate_grad)
    return logit_grad.astype(BF)


def head_kernel(
    dims,
    ranks_ref,
    lengths_ref,
    frames_ref,
    h3_ref,
    prob_ref,
    cols_ref,
    across_ref,
    returned_ref,
    place_ref,
    lines_ref,
    mine_ref,
    other_ref,
    two_grad_ref,
    logit_grad_ref,
    slots_ref,
    gain_grad_ref,
    loss_ref,
    grad_mine_ref,
    grad_other_ref,
    weight_ref,
    logits_ref,
    grad_ref,
    sems,
):
    experts, steps, shard, gain_at, tile = dims
    core = ranks_ref[2, 0]
    half = weight_ref.shape[1] // 2
    own, partner = pl.multiple_of(core * half, LANES), pl.multiple_of((1 - core) * half, LANES)
    tiles = []
    for ref, out_ref, at in ((mine_ref, grad_mine_ref, own), (other_ref, grad_other_ref, partner)):
        for k in range(half // tile):
            tiles.append((ref, out_ref, k * tile, pl.multiple_of(at + k * tile, LANES)))
    copies = start_copies(
        [
            (ref.at[:, pl.ds(near, tile)], weight_ref.at[:, pl.ds(at, tile)])
            for ref, _, near, at in tiles
        ],
        sems,
    )
    rows, width = h3_ref.shape
    vocab = weight_ref.shape[1]
    gain = lines_ref[gain_at + 4 : gain_at + 5, :]
    prob = prob_ref[...]
    chosen = chosen_lanes(cols_ref[:, 1:2], experts, prob.shape)
    gate = jnp.sum(jnp.where(chosen, prob, 0.0), axis=-1, keepdims=True)
    rows_chosen = nn(across_ref[...], returned_ref[...])
    h4 = h3_ref[...] + 0.5 * (gate * rows_chosen)
    unit, scale = norm_parts(h4)
    low = (unit * gain).astype(BF)
    turned = low.T
    top, sums = jnp.full((rows, 1), -jnp.inf, F32), jnp.zeros((rows, 1), F32)
    for copy, (_, _, _, at) in zip(copies, tiles):
        copy.wait()
        logits = nn(low, weight_ref[:, pl.ds(at, tile)])
        logits_ref[:, pl.ds(at, tile)] = logits
        higher = jnp.maximum(top, jnp.max(logits, axis=-1, keepdims=True))
        sums = sums * jnp.exp(top - higher) + jnp.sum(jnp.exp(logits - higher), axis=-1, keepdims=True)
        top = higher
    log_total = top + jnp.log(sums)
    _, _, counted_end = bounds_of(lengths_ref)
    counted = (lax.broadcasted_iota(jnp.int32, (rows, 1), 0) < counted_end).astype(F32)
    portion = counted / frames_ref[0, 0]
    target = cols_ref[:, 2:3].astype(jnp.int32)

    total, picked = jnp.zeros((rows, width), F32), jnp.zeros((rows, 1), F32)
    out_copies = []
    for i, (_, out_ref, near, at) in enumerate(tiles):
        logits = logits_ref[:, pl.ds(at, tile)]
        hit = lax.broadcasted_iota(jnp.int32, (rows, tile), 1) == (target - at)
        picked = picked + jnp.sum(jnp.where(hit, logits, 0.0), axis=-1, keepdims=True)
        guess = jnp.exp(logits - log_total)
        low_grad = (jnp.where(hit, guess - 1.0, guess) * portion).astype(BF)
        grad_ref[:, pl.ds(at, tile)] = nn(turned, low_grad).astype(BF)
        copy = pltpu.make_async_copy(
            grad_ref.at[:, pl.ds(at, tile)], out_ref.at[:, pl.ds(near, tile)], sems.at[i]
        )
        copy.start()
        out_copies.append(copy)
        total = total + nt(low_grad, weight_ref[:, pl.ds(at, tile)])
    loss = jnp.sum((log_total - picked) * counted, axis=0, keepdims=True)
    loss_ref[...] = jnp.broadcast_to(loss, loss_ref.shape)
    two_grad, gain_grad = norm_back(total, unit, scale, gain)
    two_grad_ref[...] = two_grad
    gain_grad_ref[...] = jnp.broadcast_to(gain_grad, gain_grad_ref.shape)
    half_grad = 0.5 * two_grad
    logit_grad_ref[...] = gate_backward(half_grad, prob, chosen, gate, rows_chosen)
    slots_ref[...] = nn(place_ref[...], (gate * half_grad).astype(BF)).astype(BF)
    for copy in out_copies:
        copy.wait()


def middle_backward_kernel(
    dims,
    ranks_ref,
    lengths_ref,
    two_grad_ref,
    returned_two_ref,
    across_two_ref,
    logit_two_ref,
    h1_ref,
    h2_ref,
    h3_ref,
    log_ref,
    prob_ref,
    cols_ref,
    across_ref,
    returned_ref,
    place_ref,
    extra_ref,
    lines_ref,
    mixed_ref,
    packed_ref,
    blended_ref,
    mine_ref,
    other_ref,
    one_grad_ref,
    logit_ref,
    slots_ref,
    small_ref,
    router_ref,
    grad_mine_ref,
    grad_other_ref,
    weight_ref,
    packed_grad_ref,
    padded_ref,
    padded_grad_ref,
    masks_ref,
    gated_ref,
    sums_ref,
    grad_ref,
    sems,
):
    experts, steps, shard, tap_at, taps_count, gain_at = dims
    core = ranks_ref[2, 0]
    copies = start_copies(
        shared_pairs(mine_ref, other_ref, weight_ref, ranks_ref, core, steps, shard), sems
    )
    rows, width = h1_ref.shape
    bounds = bounds_of(lengths_ref)
    gain = lambda i: lines_ref[gain_at + i : gain_at + i + 1, :]
    small_ref[...] = jnp.zeros(small_ref.shape, F32)
    unit, scale = norm_parts(h3_ref[...])
    low = (unit * gain(3)).astype(BF)
    logit_two = logit_two_ref[...]
    router_ref[...] = tn(logit_two, low)
    back = nn(across_two_ref[...], returned_two_ref[...]) + nt(logit_two, extra_ref[...])
    change, gain_grad = norm_back(back, unit, scale, gain(3))
    small_ref[taps_count : taps_count + 1, :] = gain_grad
    upstream = two_grad_ref[...] + change
    for copy in copies:
        copy.wait()
    upstream_low = upstream.astype(BF)
    unit, scale = norm_parts(h2_ref[...])
    low = (unit * gain(2)).astype(BF)
    first = nn(low, weight_ref[:, 4 * width : 5 * width])
    gate_half = jax.nn.sigmoid(nn(low, weight_ref[:, 5 * width : 6 * width]))
    clear_edges(padded_ref)
    padded_ref[TAP_PAD : TAP_PAD + rows, :] = first * gate_half
    taps = [lines_ref[tap_at + j : tap_at + j + 1, :] for j in range(taps_count)]
    masks_ref[...] = tap_masks(rows, taps_count // 2, bounds)
    mixed = mixed_ref[...]
    gate_mixed = jax.nn.sigmoid(mixed)
    active = (mixed * gate_mixed).astype(BF)
    grad_ref[:, 6 * width :] = tn(active, upstream_low).astype(BF)
    mixed_grad = (
        nt(upstream_low, weight_ref[:, 6 * width :]) * gate_mixed * (1.0 + mixed * (1.0 - gate_mixed))
    )
    clear_edges(padded_grad_ref)
    padded_grad_ref[TAP_PAD : TAP_PAD + rows, :] = mixed_grad
    conv_rows_back(padded_ref, padded_grad_ref, masks_ref, taps, gated_ref, sums_ref)
    for j in range(taps_count):
        small_ref[j : j + 1, :] = jnp.sum(sums_ref[j], axis=0, keepdims=True)
    gated_grad = gated_ref[...]
    first_low = (gated_grad * gate_half).astype(BF)
    second_low = (gated_grad * first * gate_half * (1.0 - gate_half)).astype(BF)
    grad_ref[:, 4 * width : 5 * width] = tn(low, first_low).astype(BF)
    grad_ref[:, 5 * width : 6 * width] = tn(low, second_low).astype(BF)
    back = nt(first_low, weight_ref[:, 4 * width : 5 * width]) + nt(
        second_low, weight_ref[:, 5 * width : 6 * width]
    )
    change, gain_grad = norm_back(back, unit, scale, gain(2))
    small_ref[taps_count + 1 : taps_count + 2, :] = gain_grad
    upstream = upstream + change
    upstream_low = upstream.astype(BF)
    unit, scale_norm = norm_parts(h1_ref[...])
    low = (unit * gain(1)).astype(BF)
    mixed_low = nt(upstream_low, weight_ref[:, 3 * width : 4 * width]).astype(BF)
    same = segment_of(lax.broadcasted_iota(jnp.int32, (rows, 1), 0), bounds) == segment_of(
        lax.broadcasted_iota(jnp.int32, (1, rows), 1), bounds
    )
    scale = (width // HEADS) ** (-0.5)
    for pair in range(HEADS // 2):
        at = pair * LANES
        query = packed_ref[:, at : at + LANES]
        keys = packed_ref[:, width + at : width + at + LANES]
        values = packed_ref[:, 2 * width + at : 2 * width + at + LANES]
        spread = mixed_low[:, at : at + LANES]
        held = None
        for part in range(2):
            mine = head_lanes(part, query.shape)
            head = 2 * pair + part
            scores = nt(jnp.where(mine, query, jnp.zeros_like(query)), keys) * scale
            scores = jnp.where(same, scores, MASKED)
            probs = jnp.exp(scores - log_ref[:, head : head + 1])
            weights = probs.astype(BF)
            prob_grad = nt(jnp.where(mine, spread, jnp.zeros_like(spread)), values)
            centre = jnp.sum(probs * prob_grad, axis=-1, keepdims=True)
            score_grad = (probs * (prob_grad - centre)).astype(BF)
            found = (
                tn(weights, spread),
                nn(score_grad, keys) * scale,
                tn(score_grad, query) * scale,
            )
            held = found if part == 0 else tuple(jnp.where(mine, new, old) for new, old in zip(found, held))
        packed_grad_ref[:, 2 * width + at : 2 * width + at + LANES] = held[0].astype(BF)
        packed_grad_ref[:, at : at + LANES] = held[1].astype(BF)
        packed_grad_ref[:, width + at : width + at + LANES] = held[2].astype(BF)
    grad_ref[:, 3 * width : 4 * width] = tn(blended_ref[...], upstream_low).astype(BF)
    packed_grad = packed_grad_ref[...]
    grad_ref[:, : 3 * width] = tn(low, packed_grad).astype(BF)
    out_copies = start_copies(
        shared_out_pairs(grad_ref, grad_mine_ref, grad_other_ref, ranks_ref, core, steps, shard), sems
    )
    change, gain_grad = norm_back(
        nt(packed_grad, weight_ref[:, : 3 * width]), unit, scale_norm, gain(1)
    )
    small_ref[taps_count + 2 : taps_count + 3, :] = gain_grad
    one_grad = upstream + change
    one_grad_ref[...] = one_grad
    prob = prob_ref[...]
    chosen = chosen_lanes(cols_ref[:, 0:1], 0, prob.shape)
    gate = jnp.sum(jnp.where(chosen, prob, 0.0), axis=-1, keepdims=True)
    half_grad = 0.5 * one_grad
    rows_chosen = nn(across_ref[...], returned_ref[...])
    logit_ref[...] = gate_backward(half_grad, prob, chosen, gate, rows_chosen)
    slots_ref[...] = nn(place_ref[...], (gate * half_grad).astype(BF)).astype(BF)
    for copy in out_copies:
        copy.wait()


def back_kernel(
    dims,
    one_grad_ref,
    returned_ref,
    across_ref,
    logit_ref,
    x0_ref,
    feat_ref,
    extra_ref,
    lines_ref,
    small_ref,
    router_ref,
    gain_four_ref,
    out_ref,
    lines_grad_ref,
):
    experts, tap_at, taps_count, gain_at = dims
    feats = feat_ref.shape[0]
    unit, scale = norm_parts(x0_ref[...])
    gain = lines_ref[gain_at : gain_at + 1, :]
    low = (unit * gain).astype(BF)
    logit = logit_ref[...]
    back = nn(across_ref[...], returned_ref[...]) + nt(logit, extra_ref[...])
    change, gain_grad = norm_back(back, unit, scale, gain)
    embedded_low = (one_grad_ref[...] + change).astype(BF)
    lines_grad_ref[...] = tn(logit, low) + router_ref[...]
    lines_grad_ref[2 * experts : 2 * experts + feats, :] = nn(feat_ref[...], embedded_low)
    lines_grad_ref[tap_at : tap_at + taps_count, :] = small_ref[:taps_count, :]
    lines_grad_ref[gain_at : gain_at + 1, :] = gain_grad
    lines_grad_ref[gain_at + 1 : gain_at + 2, :] = small_ref[taps_count + 2 : taps_count + 3, :]
    lines_grad_ref[gain_at + 2 : gain_at + 3, :] = small_ref[taps_count + 1 : taps_count + 2, :]
    lines_grad_ref[gain_at + 3 : gain_at + 4, :] = small_ref[taps_count : taps_count + 1, :]
    lines_grad_ref[gain_at + 4 : gain_at + 5, :] = gain_four_ref[0:1, :]
    out_ref[...] = lines_grad_ref[...].T.astype(BF)


def spec(kind):
    space = {"v": pltpu.VMEM, "s": pltpu.SMEM, "a": pl.ANY}[kind]
    return pl.BlockSpec(memory_space=space)


def shaped(shape, dtype):
    return jax.ShapeDtypeStruct(shape, dtype)


def call(kernel, name, kinds, args, outs, out_kinds, scratch=(), flops=0, moved=0):
    return pl.pallas_call(
        kernel,
        name=name,
        out_shape=tuple(outs),
        in_specs=[spec(kind) for kind in kinds],
        out_specs=tuple(spec(kind) for kind in out_kinds),
        scratch_shapes=list(scratch),
        compiler_params=pltpu.CompilerParams(vmem_limit_bytes=VMEM_BYTES),
        cost_estimate=pl.CostEstimate(flops=int(flops), bytes_accessed=int(moved), transcendentals=0),
    )(*args)


def ring_order(size):
    return list(range(0, size, 2)) + list(range(size - 1 - (size % 2), 0, -2))


def ring_pairs(size, experts):
    order = ring_order(size)
    pairs = []
    for place in range(size):
        for e in range(experts):
            step = 1 if e % 2 == 0 else -1
            pairs.append((order[place] * experts + e, order[(place + step) % size] * experts + e))
    return pairs


def rank_table(size):
    order = ring_order(size)
    where = {rank: place for place, rank in enumerate(order)}
    table = np.zeros((size, 2, size), np.int32)
    for rank in range(size):
        for core in range(2):
            step = 1 if core == 0 else -1
            for k in range(size):
                table[rank, core, k] = order[(where[rank] - step * k) % size]
    return table


def tie(value, *others):
    return lax.optimization_barrier((value, *others))[0]


def ring_step(array, pairs):
    return lax.ppermute(array, ALL, pairs)


def ring_gather(shard, pairs, size):
    chunks = [shard]
    for _ in range(size - 1):
        chunks.append(ring_step(chunks[-1], pairs))
    return chunks


def core_swap(array, experts):
    return lax.ppermute(array, "expert", [(e, e ^ 1) for e in range(experts)])


def over_chips(array, experts):
    total = array.astype(F32)
    chips = experts // 2
    for shift in range(1, chips):
        moved = lax.ppermute(
            array, "expert", [(e, (e // 2 + shift) % chips * 2 + e % 2) for e in range(experts)]
        )
        total = total + moved.astype(F32)
    return total


def swap_rows(slots, experts):
    parts = slots.reshape(experts, slots.shape[0] // experts, slots.shape[1])
    return lax.all_to_all(parts, "expert", split_axis=0, concat_axis=0, tiled=True).reshape(slots.shape)


def shared_finish(partial, experts, core):
    own = over_chips(partial, experts).astype(BF)
    far = core_swap(own, experts)
    return jnp.where(core == 0, jnp.concatenate([own, far], 1), jnp.concatenate([far, own], 1))


def shared_scatter(mine, other, pairs, size, experts, core):
    arrived = core_swap(other, experts)
    partial = (mine[0] + arrived[0]).astype(BF)
    for k in range(1, size):
        partial = ring_step(partial, pairs) + (mine[k] + arrived[k])
    return shared_finish(partial, experts, core)


def expert_scatter(chunks, pairs):
    partial = chunks[0]
    for chunk in chunks[1:]:
        partial = ring_step(partial, pairs) + chunk
    return partial


def adamw(gradient, master, moment, square, rate, decay):
    moment = BETA_ONE * moment + (1.0 - BETA_ONE) * gradient
    square = BETA_TWO * square + (1.0 - BETA_TWO) * gradient * gradient
    update = (
        moment / (1.0 - BETA_ONE**STEP) / (jnp.sqrt(square / (1.0 - BETA_TWO**STEP)) + ADAM_EPS)
    )
    return (moment, square, master - rate * (update + decay * master))


def on_device(features, lengths, routes, alignment, *weights):
    copies, masters, firsts, seconds = (weights[8 * i : 8 * i + 8] for i in range(4))
    attend_copy, output_copy, conv_copy, head_copy, extra_copy, gains_copy, up_copy, down_copy = copies
    size = lax.axis_size("dp")
    experts = lax.axis_size("expert")
    dp_at = lax.axis_index("dp")
    expert_at = lax.axis_index("expert")
    core = expert_at % 2
    row_count, feat_count = features.shape
    shard = attend_copy.shape[0]
    width = shard * size
    vocab = head_copy.shape[1]
    units = up_copy.shape[3]
    aux = extra_copy.shape[1]
    taps_count = aux - 2 * experts - feat_count
    tap_at = 2 * experts + feat_count
    gain_at = aux
    capacity = row_count * 5 // (4 * experts)
    slot_count = experts * capacity
    pairs = ring_pairs(size, experts)
    table = jnp.asarray(rank_table(size))[dp_at]
    ranks = jnp.concatenate(
        [
            lax.dynamic_index_in_dim(table, core, 0, keepdims=True),
            lax.dynamic_index_in_dim(table, 1 - core, 0, keepdims=True),
            jnp.full((1, size), core, jnp.int32),
        ]
    )

    everyone = size * experts
    gain_count = gains_copy.shape[0]
    frames_here = row_count - lengths[0, 3]
    digits = jnp.stack([frames_here // 16, frames_here % 16]).astype(BF)
    pack = jnp.concatenate(
        [
            extra_copy,
            gains_copy.T,
            jnp.broadcast_to(digits[None], (shard, 2)),
            jnp.zeros((shard, LANES - aux - gain_count - 2), BF),
        ],
        axis=1,
    )
    packs = lax.all_to_all(
        jnp.broadcast_to(pack[None], (size,) + pack.shape), "dp", split_axis=0, concat_axis=0, tiled=True
    )
    extra = packs.reshape(width, LANES)
    tops = jnp.sum(packs[:, 0].astype(F32), axis=0)
    frames = jnp.full((8, LANES), 16.0 * tops[gain_at + gain_count] + tops[gain_at + gain_count + 1])
    frames = frames + core_swap(frames, experts)
    frame_count = over_chips(frames, experts)[0, 0]

    expert_shards = [
        jnp.stack([up_copy[f, 0], down_copy[f, 0].T]) for f in range(2)
    ]
    second_chunks = ring_gather(expert_shards[1], pairs, size)
    shared = jnp.concatenate([attend_copy, output_copy, conv_copy], axis=1)
    half_shared = shared.shape[1] // 2
    shared_chunks = ring_gather(
        lax.dynamic_slice_in_dim(shared, core * half_shared, half_shared, 1), pairs, size
    )
    shared_mine = jnp.stack(shared_chunks)
    shared_other = core_swap(shared_mine, experts)
    half_vocab = vocab // 2
    head_half = lax.dynamic_slice_in_dim(head_copy, core * half_vocab, half_vocab, 1)

    square = (row_count, width)
    lanes = (row_count, LANES)
    cols, place_one, across_one, place_two, across_two = call(
        functools.partial(routing_kernel, capacity),
        "routing",
        "vv",
        (jnp.swapaxes(routes, 1, 2), alignment[None, :]),
        [shaped(lanes, F32)]
        + [shaped((slot_count, row_count), BF), shaped((row_count, slot_count), BF)] * 2,
        "vvvvv",
    )
    features_across = features.T

    def front(feat_ref, extra_ref, place_ref, *outs):
        front_kernel(experts, feat_ref, extra_ref, place_ref, gain_at, *outs)

    x0, slots_one, prob_one, lines = call(
        front,
        "front",
        "vvv",
        (features_across, extra, place_one),
        [shaped(square, F32), shaped((slot_count, width), BF), shaped(lanes, F32), shaped((LANES, width), F32)],
        "vvvv",
        flops=1e9,
        moved=4e6,
    )
    tile = 512
    expert_scratch = [
        pltpu.VMEM((2, width, units), BF),
        pltpu.SemaphoreType.DMA((units // tile, size)),
    ]
    grads_scratch = [pltpu.VMEM((2, width, units), BF), pltpu.SemaphoreType.DMA((size,))]
    tile = 512

    def expert_forward(slots, chunks):
        return call(
            functools.partial(expert_forward_kernel, size, tile),
            "expert_forward",
            "sv" + "a" * size,
            (ranks, slots, *chunks),
            [shaped(slots.shape, BF)],
            "v",
            expert_scratch,
            flops=4.0 * slot_count * width * units,
            moved=6e6,
        )[0]

    received_one = swap_rows(slots_one, experts)
    waits = {1: [extra], 4: [slots_one], 6: [received_one]}
    first_chunks = [expert_shards[0]]
    for k in range(1, size):
        first_chunks.append(ring_step(tie(first_chunks[-1], *waits.get(k, [])), pairs))
    head_mine = lax.all_gather(
        tie(head_half, first_chunks[-1], second_chunks[-1], shared_chunks[-1]), "dp", axis=0, tiled=True
    )
    returned_one = swap_rows(expert_forward(received_one, first_chunks), experts)
    copy_sems = pltpu.SemaphoreType.DMA((2 * size,))
    middle_dims = (experts, size, shard, tap_at, taps_count, gain_at)
    h1, h2, h3, logs, prob_two, slots_two, mixed, packed, blended = call(
        functools.partial(middle_forward_kernel, middle_dims),
        "middle_forward",
        "ssvvvvvvvvaa",
        (
            ranks,
            lengths,
            x0,
            prob_one,
            cols,
            across_one,
            returned_one,
            place_two,
            extra,
            lines,
            shared_mine,
            shared_other,
        ),
        [shaped(square, F32)] * 3
        + [
            shaped(lanes, F32),
            shaped(lanes, F32),
            shaped((slot_count, width), BF),
            shaped(square, F32),
            shaped((row_count, 3 * width), BF),
            shaped(square, BF),
        ],
        "vvvvvvvvv",
        [
            pltpu.VMEM((width, 7 * width), BF),
            pltpu.VMEM((row_count + 2 * TAP_PAD, width), F32),
            pltpu.VMEM(lanes, F32),
            copy_sems,
        ],
        flops=12e9,
        moved=10e6,
    )
    received_two = swap_rows(slots_two, experts)
    expert_two = expert_forward(received_two, second_chunks)
    returned_two = swap_rows(expert_two, experts)
    head_mine = tie(head_mine, expert_two)
    head_other = core_swap(head_mine, experts)
    two_grad, logit_two, grad_slots_two, gain_four, loss_part, head_grad_mine, head_grad_other = call(
        functools.partial(head_kernel, (experts, size, shard, gain_at, 2048)),
        "head",
        "sssvvvvvvvaa",
        (
            ranks,
            lengths,
            frame_count.reshape(1, 1),
            h3,
            prob_two,
            cols,
            across_two,
            returned_two,
            place_two,
            lines,
            head_mine,
            head_other,
        ),
        [
            shaped(square, F32),
            shaped(lanes, BF),
            shaped((slot_count, width), BF),
            shaped((8, width), F32),
            shaped((8, LANES), F32),
            shaped((width, half_vocab), BF),
            shaped((width, half_vocab), BF),
        ],
        "vvvvvaa",
        [
            pltpu.VMEM((width, vocab), BF),
            pltpu.VMEM((row_count, vocab), F32),
            pltpu.VMEM((width, vocab), BF),
            copy_sems,
        ],
        flops=20e9,
        moved=20e6,
    )

    def expert_backward(slots, grads, chunks):
        back, active, hidden = call(
            functools.partial(expert_backward_kernel, size, tile),
            "expert_backward",
            "svv" + "a" * size,
            (ranks, slots, grads, *chunks),
            [shaped(slots.shape, BF), shaped((slot_count, units), BF), shaped((slot_count, units), BF)],
            "vvv",
            expert_scratch,
            flops=6.0 * slot_count * width * units,
            moved=12e6,
        )
        sums = call(
            functools.partial(expert_grads_kernel, size, tile),
            "expert_grads",
            "svvvv",
            (ranks, slots, grads, active, hidden),
            [shaped((2, shard, units), BF)] * size,
            "a" * size,
            grads_scratch,
            flops=4.0 * slot_count * width * units,
            moved=10e6,
        )
        return back, sums

    head_total = head_grad_mine + core_swap(head_grad_other, experts)
    out_grad_two = tie(swap_rows(grad_slots_two, experts), head_total)
    head_part = lax.psum_scatter(head_total, "dp", scatter_dimension=0, tiled=True)
    back_two, sums_two = expert_backward(received_two, out_grad_two, second_chunks)
    slot_grad_two = tie(swap_rows(back_two, experts), sums_two[0])
    one_grad, logit_one, grad_slots_one, small, router_two, mid_grad_mine, mid_grad_other = call(
        functools.partial(middle_backward_kernel, middle_dims),
        "middle_backward",
        "ss" + "v" * 18 + "aa",
        (
            ranks,
            lengths,
            two_grad,
            slot_grad_two,
            across_two,
            logit_two,
            h1,
            h2,
            h3,
            logs,
            prob_one,
            cols,
            across_one,
            returned_one,
            place_one,
            extra,
            lines,
            mixed,
            packed,
            blended,
            shared_mine,
            shared_other,
        ),
        [
            shaped(square, F32),
            shaped(lanes, BF),
            shaped((slot_count, width), BF),
            shaped((24, width), F32),
            shaped((LANES, width), F32),
            shaped((size, shard, half_shared), BF),
            shaped((size, shard, half_shared), BF),
        ],
        "vvvvvaa",
        [
            pltpu.VMEM((width, 7 * width), BF),
            pltpu.VMEM((row_count, 3 * width), BF),
            pltpu.VMEM((row_count + 2 * TAP_PAD, width), F32),
            pltpu.VMEM((row_count + 2 * TAP_PAD, width), F32),
            pltpu.VMEM(lanes, F32),
            pltpu.VMEM(square, F32),
            pltpu.VMEM((16, 8, width), F32),
            pltpu.VMEM((width, 7 * width), BF),
            copy_sems,
        ],
        flops=25e9,
        moved=20e6,
    )
    out_grad_one = swap_rows(grad_slots_one, experts)
    back_one, sums_one = expert_backward(received_one, out_grad_one, first_chunks)
    slot_grad_one = tie(swap_rows(back_one, experts), sums_one[0])
    (extra_grad,) = call(
        functools.partial(back_kernel, (experts, tap_at, taps_count, gain_at)),
        "back",
        "v" * 11,
        (
            one_grad,
            slot_grad_one,
            across_one,
            logit_one,
            x0,
            features_across,
            extra,
            lines,
            small,
            router_two,
            gain_four,
        ),
        [shaped((width, LANES), BF)],
        "v",
        [pltpu.VMEM((LANES, width), F32)],
        flops=2e9,
        moved=5e6,
    )

    head_sum = shared_finish(head_part, experts, core).astype(F32)
    sums_two = expert_scatter(sums_two, pairs)
    mid_sum = shared_scatter(mid_grad_mine, mid_grad_other, pairs, size, experts, core).astype(F32)
    sums_one = expert_scatter(sums_one, pairs)
    spread = jnp.broadcast_to(
        extra_grad.reshape(size, 1, shard, LANES), (size, experts, shard, LANES)
    ).reshape(everyone, shard, LANES)
    small_sum = jnp.sum(
        lax.all_to_all(spread, ALL, split_axis=0, concat_axis=0, tiled=True).astype(F32), axis=0
    )
    extra_sum = small_sum[:, :aux]
    gains_sum = small_sum[:, aux : aux + gains_copy.shape[0]].T
    attend_sum = mid_sum[:, : 3 * width]
    output_sum = mid_sum[:, 3 * width : 4 * width]
    conv_sum = mid_sum[:, 4 * width :]
    up_sum = jnp.stack([sums_one[0], sums_two[0]])[:, None].astype(F32)
    down_sum = jnp.stack([sums_one[1], sums_two[1]])[:, None].astype(F32)
    shared_squares = jnp.float32(0.0)
    for member in (mid_sum, head_sum, extra_sum, gains_sum):
        shared_squares = shared_squares + jnp.sum(member * member)
    expert_squares = jnp.sum(up_sum * up_sum) + jnp.sum(down_sum * down_sum)
    local_squares = jnp.where(expert_at == 0, shared_squares, 0.0) + expert_squares
    totals = jnp.stack([local_squares, loss_part[0, 0]])
    totals = jnp.sum(
        lax.all_to_all(
            jnp.broadcast_to(totals[None, :, None], (everyone, 2, LANES)),
            ALL,
            split_axis=0,
            concat_axis=0,
            tiled=True,
        )[:, :, 0],
        axis=0,
    )
    global_norm = jnp.sqrt(totals[0])
    loss_sum = totals[1]
    factor = jnp.minimum(1.0, 0.1 * math.sqrt(width / (row_count * everyone)) / global_norm)
    gradients = (attend_sum, output_sum, conv_sum, head_sum, extra_sum, gains_sum, up_sum, down_sum)
    turned = lambda arrays: arrays[:7] + (jnp.swapaxes(arrays[7], 2, 3),)
    results = [
        adamw(gradient * factor, master, moment, second, rate, decay)
        for gradient, master, moment, second, rate, decay in zip(
            gradients, turned(masters), turned(firsts), turned(seconds), STEP_RATES, DECAYS
        )
    ]
    results[7] = tuple(jnp.swapaxes(member, 2, 3) for member in results[7])
    return (
        loss_sum,
        frame_count,
        global_norm,
        *(result[0] for result in results),
        *(result[1] for result in results),
        *(result[2] for result in results),
    )


def solution(mesh):
    weight_specs = (
        P("dp", None),
        P("dp", None),
        P("dp", None),
        P("dp", None),
        P("dp", None),
        P(None, "dp"),
        P(None, "expert", "dp", None),
        P(None, "expert", None, "dp"),
    )
    return jax.shard_map(
        on_device,
        mesh=mesh,
        in_specs=(
            P(("dp", "expert"), None),
            P(("dp", "expert"), None),
            P(None, ("dp", "expert"), None),
            P(("dp", "expert")),
        )
        + weight_specs * 4,
        out_specs=(P(), P(), P()) + weight_specs * 3,
        check_vma=False,
    )
```

```python
import functools
import math

import jax
import jax.numpy as jnp
import numpy as np
from jax import lax
from jax.experimental import pallas as pl
from jax.experimental.pallas import tpu as pltpu
from jax.sharding import PartitionSpec as P

HEADS = 8
STEP = 5
NORM_EPS = 1e-05
ADAM_EPS = 1e-08
BETA_ONE = 0.5
BETA_TWO = 0.5
MASKED = -1000000000.0
STEP_RATES = (0.02, 0.2, 0.02, 0.05, 0.05, 0.5, 0.02, 0.1)
DECAYS = (0.01, 0.01, 0.01, 0.01, 0.01, 0.0, 0.01, 0.01)

BF = jnp.bfloat16
F32 = jnp.float32
ALL = ("dp", "expert")
VMEM_BYTES = 56 * 1024 * 1024
LANES = 128
TAP_PAD = 16
TAP_ROWS = 256


def nn(left, right):
    return jnp.dot(left, right, preferred_element_type=F32)


def nt(left, right):
    return lax.dot_general(left, right, (((1,), (1,)), ((), ())), preferred_element_type=F32)


def tn(left, right):
    return lax.dot_general(left, right, (((0,), (0,)), ((), ())), preferred_element_type=F32)


def norm_parts(values):
    centred = values - jnp.mean(values, axis=-1, keepdims=True)
    scale = lax.rsqrt(jnp.mean(centred * centred, axis=-1, keepdims=True) + NORM_EPS)
    return centred * scale, scale


def norm_back(grad, unit, scale, gain_row):
    weighted = grad * gain_row
    mean = jnp.mean(weighted, axis=-1, keepdims=True)
    along = jnp.mean(weighted * unit, axis=-1, keepdims=True)
    gain_grad = jnp.sum(grad * unit, axis=0, keepdims=True)
    return scale * (weighted - mean - unit * along), gain_grad


def lane_softmax(logits, first, count):
    lane = lax.broadcasted_iota(jnp.int32, logits.shape, 1)
    inside = (lane >= first) & (lane < first + count)
    logits = jnp.where(inside, logits, -jnp.inf)
    weight = jnp.exp(logits - jnp.max(logits, axis=-1, keepdims=True))
    return weight / jnp.sum(weight, axis=-1, keepdims=True)


def chosen_lanes(route_col, first, shape):
    lane = lax.broadcasted_iota(jnp.int32, shape, 1)
    return lane == (route_col.astype(jnp.int32) + first)


def bounds_of(lengths_ref):
    first = lengths_ref[0, 0]
    second = first + lengths_ref[0, 1]
    return first, second, second + lengths_ref[0, 2]


def segment_of(places, bounds):
    total = jnp.zeros(places.shape, jnp.int32)
    for bound in bounds:
        total = total + (places >= bound).astype(jnp.int32)
    return total


def tap_masks(rows, half_span, bounds):
    place = lax.broadcasted_iota(jnp.int32, (rows, LANES), 0)
    lane = lax.broadcasted_iota(jnp.int32, (rows, LANES), 1)
    same = segment_of(place, bounds) == segment_of(place + lane - half_span, bounds)
    return same.astype(F32)


def start_copies(pairs, sems):
    copies = [pltpu.make_async_copy(src, dst, sems.at[i]) for i, (src, dst) in enumerate(pairs)]
    for copy in copies:
        copy.start()
    return copies


def rows_at(rank, rows):
    return pl.ds(pl.multiple_of(rank * rows, rows), rows)


def shared_pairs(mine_ref, other_ref, full_ref, ranks_ref, core, steps, rows):
    width = mine_ref.shape[-1]
    own = pl.ds(pl.multiple_of(core * width, LANES), width)
    far = pl.ds(pl.multiple_of((1 - core) * width, LANES), width)
    pairs = []
    for k in range(steps):
        pairs.append((mine_ref.at[k], full_ref.at[rows_at(ranks_ref[0, k], rows), own]))
        pairs.append((other_ref.at[k], full_ref.at[rows_at(ranks_ref[1, k], rows), far]))
    return pairs


def shared_out_pairs(full_ref, mine_ref, other_ref, ranks_ref, core, steps, rows):
    width = mine_ref.shape[-1]
    own = pl.ds(pl.multiple_of(core * width, LANES), width)
    far = pl.ds(pl.multiple_of((1 - core) * width, LANES), width)
    pairs = []
    for k in range(steps):
        later = (k + 1) % steps
        pairs.append((full_ref.at[rows_at(ranks_ref[0, later], rows), own], mine_ref.at[k]))
        pairs.append((full_ref.at[rows_at(ranks_ref[1, later], rows), far], other_ref.at[k]))
    return pairs


def half_pairs(mine_ref, other_ref, full_ref, core):
    width = mine_ref.shape[-1]
    own = pl.ds(pl.multiple_of(core * width, LANES), width)
    partner = pl.ds(pl.multiple_of((1 - core) * width, LANES), width)
    return [(mine_ref, full_ref.at[:, own]), (other_ref, full_ref.at[:, partner])]


def routing_kernel(capacity, routes_ref, align_ref, cols_ref, *place_refs):
    rows = routes_ref.shape[2]
    before = (
        lax.broadcasted_iota(jnp.int32, (rows, rows), 0)
        < lax.broadcasted_iota(jnp.int32, (rows, rows), 1)
    ).astype(BF)
    kept = []
    slots = []
    for f in range(2):
        route_row = routes_ref[f]
        named = lax.broadcasted_iota(jnp.int32, (16, rows), 0) == route_row
        counts = nn(named.astype(BF), before)
        rank = jnp.sum(jnp.where(named, counts, 0.0), axis=0, keepdims=True)
        slots.append(route_row.astype(F32) * capacity + rank)
        kept.append(route_row.astype(F32))
    lines = jnp.concatenate(
        kept + [align_ref[...].astype(F32)] + slots + [jnp.zeros((LANES - 5, rows), F32)], axis=0
    )
    cols = lines.T
    cols_ref[...] = cols
    for f in range(2):
        down_ref, across_ref = place_refs[2 * f], place_refs[2 * f + 1]
        slot_count = down_ref.shape[0]
        slot_row = slots[f].astype(jnp.int32)
        slot_col = cols[:, 3 + f : 4 + f].astype(jnp.int32)
        down_ref[...] = (
            lax.broadcasted_iota(jnp.int32, (slot_count, rows), 0) == slot_row
        ).astype(BF)
        across_ref[...] = (
            lax.broadcasted_iota(jnp.int32, (rows, slot_count), 1) == slot_col
        ).astype(BF)


def front_kernel(experts, feat_ref, extra_ref, place_ref, gain_at, x0_ref, slots_ref, prob_ref, lines_ref):
    extra = extra_ref[...]
    lines_ref[...] = extra.astype(F32).T
    feats = feat_ref.shape[0]
    table = lines_ref[2 * experts : 2 * experts + feats, :].astype(BF)
    embedded = tn(feat_ref[...], table)
    x0_ref[...] = embedded
    unit, _ = norm_parts(embedded)
    low = (unit * lines_ref[gain_at : gain_at + 1, :]).astype(BF)
    prob_ref[...] = lane_softmax(nn(low, extra), 0, experts)
    slots_ref[...] = nn(place_ref[...], low).astype(BF)


def load_experts(tile, ranks_ref, chunk_refs, weight_ref, sems):
    rows = chunk_refs[0].shape[1]
    groups = []
    for i in range(weight_ref.shape[2] // tile):
        columns = pl.ds(i * tile, tile)
        pairs = [
            (chunk.at[:, :, columns], weight_ref.at[:, rows_at(ranks_ref[0, k], rows), columns])
            for k, chunk in enumerate(chunk_refs)
        ]
        groups.append(start_copies(pairs, sems.at[i]))
    return groups


def expert_forward_kernel(steps, tile, ranks_ref, slots_ref, *refs):
    chunk_refs = refs[:steps]
    out_ref, weight_ref, sems = refs[steps:]
    groups = load_experts(tile, ranks_ref, chunk_refs, weight_ref, sems)
    slots = slots_ref[...]
    total = jnp.zeros(out_ref.shape, F32)
    for at in range(0, weight_ref.shape[2], tile):
        for copy in groups[at // tile]:
            copy.wait()
        hidden = nn(slots, weight_ref[0, :, at : at + tile])
        active = (hidden * jax.nn.sigmoid(hidden)).astype(BF)
        total = total + nt(active, weight_ref[1, :, at : at + tile])
    out_ref[...] = total.astype(BF)


def expert_backward_kernel(steps, tile, ranks_ref, slots_ref, grad_ref, *refs):
    chunk_refs = refs[:steps]
    back_ref, active_ref, hidden_ref, weight_ref, sems = refs[steps:]
    groups = load_experts(tile, ranks_ref, chunk_refs, weight_ref, sems)
    slots = slots_ref[...]
    grad = grad_ref[...]
    total = jnp.zeros(back_ref.shape, F32)
    for at in range(0, weight_ref.shape[2], tile):
        here = slice(at, at + tile)
        for copy in groups[at // tile]:
            copy.wait()
        hidden = nn(slots, weight_ref[0, :, here])
        gate = jax.nn.sigmoid(hidden)
        active_ref[:, here] = (hidden * gate).astype(BF)
        hidden_grad = (nn(grad, weight_ref[1, :, here]) * gate * (1.0 + hidden * (1.0 - gate))).astype(BF)
        hidden_ref[:, here] = hidden_grad
        total = total + nt(hidden_grad, weight_ref[0, :, here])
    back_ref[...] = total.astype(BF)


def expert_grads_kernel(steps, tile, ranks_ref, slots_ref, grad_ref, active_ref, hidden_ref, *refs):
    out_refs = refs[:steps]
    sum_ref, sems = refs[steps:]
    slots = slots_ref[...].T
    grad = grad_ref[...].T
    for at in range(0, active_ref.shape[1], tile):
        here = slice(at, at + tile)
        sum_ref[0, :, here] = nn(slots, hidden_ref[:, here]).astype(BF)
        sum_ref[1, :, here] = nn(grad, active_ref[:, here]).astype(BF)
    rows = out_refs[0].shape[1]
    pairs = [
        (sum_ref.at[:, rows_at(ranks_ref[0, (k + 1) % steps], rows), :], out)
        for k, out in enumerate(out_refs)
    ]
    for copy in start_copies(pairs, sems):
        copy.wait()


def head_lanes(pair_at, shape):
    lane = lax.broadcasted_iota(jnp.int32, shape, 1)
    return (lane < LANES // 2) if pair_at == 0 else (lane >= LANES // 2)


def tap_window(padded_ref, base, half_span):
    start = base + TAP_PAD - half_span
    return lambda j: padded_ref[start + j : start + j + TAP_ROWS, :]


def clear_edges(padded_ref):
    edge = jnp.zeros((TAP_PAD, padded_ref.shape[1]), F32)
    padded_ref[:TAP_PAD, :] = edge
    padded_ref[padded_ref.shape[0] - TAP_PAD :, :] = edge


def conv_rows(padded_ref, masks_ref, taps, out_ref):
    count = len(taps)

    for base in range(0, masks_ref.shape[0], TAP_ROWS):
        shifted = tap_window(padded_ref, base, count // 2)
        masks = masks_ref[pl.ds(base, TAP_ROWS), :]
        total = jnp.zeros((TAP_ROWS, padded_ref.shape[1]), F32)
        for j in range(count):
            total = total + shifted(j) * masks[:, j : j + 1] * taps[j]
        out_ref[pl.ds(base, TAP_ROWS), :] = total


def conv_rows_back(padded_ref, padded_grad_ref, masks_ref, taps, out_ref, sums_ref):
    count = len(taps)
    width = padded_ref.shape[1]
    sums_ref[...] = jnp.zeros(sums_ref.shape, F32)

    for base in range(0, masks_ref.shape[0], TAP_ROWS):
        values = tap_window(padded_ref, base, count // 2)
        grads = tap_window(padded_grad_ref, base, count // 2)
        masks = masks_ref[pl.ds(base, TAP_ROWS), :]
        here = grads(count // 2)
        total = jnp.zeros((TAP_ROWS, width), F32)
        for j in range(count):
            mask = masks[:, j : j + 1]
            total = total + grads(j) * mask * taps[count - 1 - j]
            part = values(j) * mask * here
            sums_ref[j] += jnp.sum(part.reshape(TAP_ROWS // 8, 8, width), axis=0)
        out_ref[pl.ds(base, TAP_ROWS), :] = total


def middle_forward_kernel(
    dims,
    ranks_ref,
    lengths_ref,
    x0_ref,
    prob_ref,
    cols_ref,
    across_ref,
    returned_ref,
    place_ref,
    extra_ref,
    lines_ref,
    mine_ref,
    other_ref,
    h1_ref,
    h2_ref,
    h3_ref,
    log_ref,
    prob_two_ref,
    slots_ref,
    mixed_ref,
    packed_ref,
    blended_ref,
    weight_ref,
    padded_ref,
    masks_ref,
    sems,
):
    experts, steps, shard, tap_at, taps_count, gain_at = dims
    core = ranks_ref[2, 0]
    copies = start_copies(
        shared_pairs(mine_ref, other_ref, weight_ref, ranks_ref, core, steps, shard), sems
    )
    rows, width = x0_ref.shape
    bounds = bounds_of(lengths_ref)
    gain = lambda i: lines_ref[gain_at + i : gain_at + i + 1, :]
    prob = prob_ref[...]
    gate = jnp.sum(
        jnp.where(chosen_lanes(cols_ref[:, 0:1], 0, prob.shape), prob, 0.0), axis=-1, keepdims=True
    )
    h1 = x0_ref[...] + 0.5 * (gate * nn(across_ref[...], returned_ref[...]))
    h1_ref[...] = h1
    unit, _ = norm_parts(h1)
    low = (unit * gain(1)).astype(BF)
    for copy in copies:
        copy.wait()
    packed_ref[...] = nn(low, weight_ref[:, : 3 * width]).astype(BF)
    same = segment_of(lax.broadcasted_iota(jnp.int32, (rows, 1), 0), bounds) == segment_of(
        lax.broadcasted_iota(jnp.int32, (1, rows), 1), bounds
    )
    scale = (width // HEADS) ** (-0.5)
    log_lane = lax.broadcasted_iota(jnp.int32, (rows, LANES), 1)
    logs = jnp.zeros((rows, LANES), F32)
    for pair in range(HEADS // 2):
        at = pair * LANES
        query = packed_ref[:, at : at + LANES]
        keys = packed_ref[:, width + at : width + at + LANES]
        values = packed_ref[:, 2 * width + at : 2 * width + at + LANES]
        mixed = None
        for half in range(2):
            mine = head_lanes(half, query.shape)
            scores = nt(jnp.where(mine, query, jnp.zeros_like(query)), keys) * scale
            scores = jnp.where(same, scores, MASKED)
            top = jnp.max(scores, axis=-1, keepdims=True)
            exponent = jnp.exp(scores - top)
            sums = jnp.sum(exponent, axis=-1, keepdims=True)
            weights = (exponent * (1.0 / sums)).astype(BF)
            part = nn(weights, values)
            mixed = part if half == 0 else jnp.where(mine, part, mixed)
            logs = jnp.where(log_lane == 2 * pair + half, top + jnp.log(sums), logs)
        blended_ref[:, at : at + LANES] = mixed.astype(BF)
    log_ref[...] = logs
    h2 = h1 + nn(blended_ref[...], weight_ref[:, 3 * width : 4 * width])
    h2_ref[...] = h2
    unit, _ = norm_parts(h2)
    low = (unit * gain(2)).astype(BF)
    first = nn(low, weight_ref[:, 4 * width : 5 * width])
    second = nn(low, weight_ref[:, 5 * width : 6 * width])
    clear_edges(padded_ref)
    padded_ref[TAP_PAD : TAP_PAD + rows, :] = first * jax.nn.sigmoid(second)
    masks_ref[...] = tap_masks(rows, taps_count // 2, bounds)
    taps = [lines_ref[tap_at + j : tap_at + j + 1, :] for j in range(taps_count)]
    conv_rows(padded_ref, masks_ref, taps, mixed_ref)
    mixed = mixed_ref[...]
    active = (mixed * jax.nn.sigmoid(mixed)).astype(BF)
    h3 = h2 + nn(active, weight_ref[:, 6 * width :])
    h3_ref[...] = h3
    unit, _ = norm_parts(h3)
    low = (unit * gain(3)).astype(BF)
    prob_two_ref[...] = lane_softmax(nn(low, extra_ref[...]), experts, experts)
    slots_ref[...] = nn(place_ref[...], low).astype(BF)


def gate_backward(grad, prob, chosen, gate, rows_chosen):
    gate_grad = jnp.sum(grad * rows_chosen, axis=-1, keepdims=True)
    logit_grad = prob * (jnp.where(chosen, gate_grad, 0.0) - gate * gate_grad)
    return logit_grad.astype(BF)


def head_kernel(
    dims,
    ranks_ref,
    lengths_ref,
    frames_ref,
    h3_ref,
    prob_ref,
    cols_ref,
    across_ref,
    returned_ref,
    place_ref,
    lines_ref,
    mine_ref,
    other_ref,
    two_grad_ref,
    logit_grad_ref,
    slots_ref,
    gain_grad_ref,
    loss_ref,
    grad_mine_ref,
    grad_other_ref,
    weight_ref,
    logits_ref,
    grad_ref,
    sems,
):
    experts, steps, shard, gain_at, tile = dims
    core = ranks_ref[2, 0]
    half = weight_ref.shape[1] // 2
    own, partner = pl.multiple_of(core * half, LANES), pl.multiple_of((1 - core) * half, LANES)
    tiles = []
    for ref, out_ref, at in ((mine_ref, grad_mine_ref, own), (other_ref, grad_other_ref, partner)):
        for k in range(half // tile):
            tiles.append((ref, out_ref, k * tile, pl.multiple_of(at + k * tile, LANES)))
    copies = start_copies(
        [
            (ref.at[:, pl.ds(near, tile)], weight_ref.at[:, pl.ds(at, tile)])
            for ref, _, near, at in tiles
        ],
        sems,
    )
    rows, width = h3_ref.shape
    vocab = weight_ref.shape[1]
    gain = lines_ref[gain_at + 4 : gain_at + 5, :]
    prob = prob_ref[...]
    chosen = chosen_lanes(cols_ref[:, 1:2], experts, prob.shape)
    gate = jnp.sum(jnp.where(chosen, prob, 0.0), axis=-1, keepdims=True)
    rows_chosen = nn(across_ref[...], returned_ref[...])
    h4 = h3_ref[...] + 0.5 * (gate * rows_chosen)
    unit, scale = norm_parts(h4)
    low = (unit * gain).astype(BF)
    turned = low.T
    top, sums = jnp.full((rows, 1), -jnp.inf, F32), jnp.zeros((rows, 1), F32)
    for copy, (_, _, _, at) in zip(copies, tiles):
        copy.wait()
        logits = nn(low, weight_ref[:, pl.ds(at, tile)])
        logits_ref[:, pl.ds(at, tile)] = logits
        higher = jnp.maximum(top, jnp.max(logits, axis=-1, keepdims=True))
        sums = sums * jnp.exp(top - higher) + jnp.sum(jnp.exp(logits - higher), axis=-1, keepdims=True)
        top = higher
    log_total = top + jnp.log(sums)
    _, _, counted_end = bounds_of(lengths_ref)
    counted = (lax.broadcasted_iota(jnp.int32, (rows, 1), 0) < counted_end).astype(F32)
    portion = counted / frames_ref[0, 0]
    target = cols_ref[:, 2:3].astype(jnp.int32)

    total, picked = jnp.zeros((rows, width), F32), jnp.zeros((rows, 1), F32)
    out_copies = []
    for i, (_, out_ref, near, at) in enumerate(tiles):
        logits = logits_ref[:, pl.ds(at, tile)]
        hit = lax.broadcasted_iota(jnp.int32, (rows, tile), 1) == (target - at)
        picked = picked + jnp.sum(jnp.where(hit, logits, 0.0), axis=-1, keepdims=True)
        guess = jnp.exp(logits - log_total)
        low_grad = (jnp.where(hit, guess - 1.0, guess) * portion).astype(BF)
        grad_ref[:, pl.ds(at, tile)] = nn(turned, low_grad).astype(BF)
        copy = pltpu.make_async_copy(
            grad_ref.at[:, pl.ds(at, tile)], out_ref.at[:, pl.ds(near, tile)], sems.at[i]
        )
        copy.start()
        out_copies.append(copy)
        total = total + nt(low_grad, weight_ref[:, pl.ds(at, tile)])
    loss = jnp.sum((log_total - picked) * counted, axis=0, keepdims=True)
    loss_ref[...] = jnp.broadcast_to(loss, loss_ref.shape)
    two_grad, gain_grad = norm_back(total, unit, scale, gain)
    two_grad_ref[...] = two_grad
    gain_grad_ref[...] = jnp.broadcast_to(gain_grad, gain_grad_ref.shape)
    half_grad = 0.5 * two_grad
    logit_grad_ref[...] = gate_backward(half_grad, prob, chosen, gate, rows_chosen)
    slots_ref[...] = nn(place_ref[...], (gate * half_grad).astype(BF)).astype(BF)
    for copy in out_copies:
        copy.wait()


def middle_backward_kernel(
    dims,
    ranks_ref,
    lengths_ref,
    two_grad_ref,
    returned_two_ref,
    across_two_ref,
    logit_two_ref,
    h1_ref,
    h2_ref,
    h3_ref,
    log_ref,
    prob_ref,
    cols_ref,
    across_ref,
    returned_ref,
    place_ref,
    extra_ref,
    lines_ref,
    mixed_ref,
    packed_ref,
    blended_ref,
    mine_ref,
    other_ref,
    one_grad_ref,
    logit_ref,
    slots_ref,
    small_ref,
    router_ref,
    grad_mine_ref,
    grad_other_ref,
    weight_ref,
    packed_grad_ref,
    padded_ref,
    padded_grad_ref,
    masks_ref,
    gated_ref,
    sums_ref,
    grad_ref,
    sems,
):
    experts, steps, shard, tap_at, taps_count, gain_at = dims
    core = ranks_ref[2, 0]
    copies = start_copies(
        shared_pairs(mine_ref, other_ref, weight_ref, ranks_ref, core, steps, shard), sems
    )
    rows, width = h1_ref.shape
    bounds = bounds_of(lengths_ref)
    gain = lambda i: lines_ref[gain_at + i : gain_at + i + 1, :]
    small_ref[...] = jnp.zeros(small_ref.shape, F32)
    unit, scale = norm_parts(h3_ref[...])
    low = (unit * gain(3)).astype(BF)
    logit_two = logit_two_ref[...]
    router_ref[...] = tn(logit_two, low)
    back = nn(across_two_ref[...], returned_two_ref[...]) + nt(logit_two, extra_ref[...])
    change, gain_grad = norm_back(back, unit, scale, gain(3))
    small_ref[taps_count : taps_count + 1, :] = gain_grad
    upstream = two_grad_ref[...] + change
    for copy in copies:
        copy.wait()
    upstream_low = upstream.astype(BF)
    unit, scale = norm_parts(h2_ref[...])
    low = (unit * gain(2)).astype(BF)
    first = nn(low, weight_ref[:, 4 * width : 5 * width])
    gate_half = jax.nn.sigmoid(nn(low, weight_ref[:, 5 * width : 6 * width]))
    clear_edges(padded_ref)
    padded_ref[TAP_PAD : TAP_PAD + rows, :] = first * gate_half
    taps = [lines_ref[tap_at + j : tap_at + j + 1, :] for j in range(taps_count)]
    masks_ref[...] = tap_masks(rows, taps_count // 2, bounds)
    mixed = mixed_ref[...]
    gate_mixed = jax.nn.sigmoid(mixed)
    active = (mixed * gate_mixed).astype(BF)
    grad_ref[:, 6 * width :] = tn(active, upstream_low).astype(BF)
    mixed_grad = (
        nt(upstream_low, weight_ref[:, 6 * width :]) * gate_mixed * (1.0 + mixed * (1.0 - gate_mixed))
    )
    clear_edges(padded_grad_ref)
    padded_grad_ref[TAP_PAD : TAP_PAD + rows, :] = mixed_grad
    conv_rows_back(padded_ref, padded_grad_ref, masks_ref, taps, gated_ref, sums_ref)
    for j in range(taps_count):
        small_ref[j : j + 1, :] = jnp.sum(sums_ref[j], axis=0, keepdims=True)
    gated_grad = gated_ref[...]
    first_low = (gated_grad * gate_half).astype(BF)
    second_low = (gated_grad * first * gate_half * (1.0 - gate_half)).astype(BF)
    grad_ref[:, 4 * width : 5 * width] = tn(low, first_low).astype(BF)
    grad_ref[:, 5 * width : 6 * width] = tn(low, second_low).astype(BF)
    back = nt(first_low, weight_ref[:, 4 * width : 5 * width]) + nt(
        second_low, weight_ref[:, 5 * width : 6 * width]
    )
    change, gain_grad = norm_back(back, unit, scale, gain(2))
    small_ref[taps_count + 1 : taps_count + 2, :] = gain_grad
    upstream = upstream + change
    upstream_low = upstream.astype(BF)
    unit, scale_norm = norm_parts(h1_ref[...])
    low = (unit * gain(1)).astype(BF)
    mixed_low = nt(upstream_low, weight_ref[:, 3 * width : 4 * width]).astype(BF)
    same = segment_of(lax.broadcasted_iota(jnp.int32, (rows, 1), 0), bounds) == segment_of(
        lax.broadcasted_iota(jnp.int32, (1, rows), 1), bounds
    )
    scale = (width // HEADS) ** (-0.5)
    for pair in range(HEADS // 2):
        at = pair * LANES
        query = packed_ref[:, at : at + LANES]
        keys = packed_ref[:, width + at : width + at + LANES]
        values = packed_ref[:, 2 * width + at : 2 * width + at + LANES]
        spread = mixed_low[:, at : at + LANES]
        held = None
        for part in range(2):
            mine = head_lanes(part, query.shape)
            head = 2 * pair + part
            scores = nt(jnp.where(mine, query, jnp.zeros_like(query)), keys) * scale
            scores = jnp.where(same, scores, MASKED)
            probs = jnp.exp(scores - log_ref[:, head : head + 1])
            weights = probs.astype(BF)
            prob_grad = nt(jnp.where(mine, spread, jnp.zeros_like(spread)), values)
            centre = jnp.sum(probs * prob_grad, axis=-1, keepdims=True)
            score_grad = (probs * (prob_grad - centre)).astype(BF)
            found = (
                tn(weights, spread),
                nn(score_grad, keys) * scale,
                tn(score_grad, query) * scale,
            )
            held = found if part == 0 else tuple(jnp.where(mine, new, old) for new, old in zip(found, held))
        packed_grad_ref[:, 2 * width + at : 2 * width + at + LANES] = held[0].astype(BF)
        packed_grad_ref[:, at : at + LANES] = held[1].astype(BF)
        packed_grad_ref[:, width + at : width + at + LANES] = held[2].astype(BF)
    grad_ref[:, 3 * width : 4 * width] = tn(blended_ref[...], upstream_low).astype(BF)
    packed_grad = packed_grad_ref[...]
    grad_ref[:, : 3 * width] = tn(low, packed_grad).astype(BF)
    out_copies = start_copies(
        shared_out_pairs(grad_ref, grad_mine_ref, grad_other_ref, ranks_ref, core, steps, shard), sems
    )
    change, gain_grad = norm_back(
        nt(packed_grad, weight_ref[:, : 3 * width]), unit, scale_norm, gain(1)
    )
    small_ref[taps_count + 2 : taps_count + 3, :] = gain_grad
    one_grad = upstream + change
    one_grad_ref[...] = one_grad
    prob = prob_ref[...]
    chosen = chosen_lanes(cols_ref[:, 0:1], 0, prob.shape)
    gate = jnp.sum(jnp.where(chosen, prob, 0.0), axis=-1, keepdims=True)
    half_grad = 0.5 * one_grad
    rows_chosen = nn(across_ref[...], returned_ref[...])
    logit_ref[...] = gate_backward(half_grad, prob, chosen, gate, rows_chosen)
    slots_ref[...] = nn(place_ref[...], (gate * half_grad).astype(BF)).astype(BF)
    for copy in out_copies:
        copy.wait()


def back_kernel(
    dims,
    one_grad_ref,
    returned_ref,
    across_ref,
    logit_ref,
    x0_ref,
    feat_ref,
    extra_ref,
    lines_ref,
    small_ref,
    router_ref,
    gain_four_ref,
    out_ref,
    lines_grad_ref,
):
    experts, tap_at, taps_count, gain_at = dims
    feats = feat_ref.shape[0]
    unit, scale = norm_parts(x0_ref[...])
    gain = lines_ref[gain_at : gain_at + 1, :]
    low = (unit * gain).astype(BF)
    logit = logit_ref[...]
    back = nn(across_ref[...], returned_ref[...]) + nt(logit, extra_ref[...])
    change, gain_grad = norm_back(back, unit, scale, gain)
    embedded_low = (one_grad_ref[...] + change).astype(BF)
    lines_grad_ref[...] = tn(logit, low) + router_ref[...]
    lines_grad_ref[2 * experts : 2 * experts + feats, :] = nn(feat_ref[...], embedded_low)
    lines_grad_ref[tap_at : tap_at + taps_count, :] = small_ref[:taps_count, :]
    lines_grad_ref[gain_at : gain_at + 1, :] = gain_grad
    lines_grad_ref[gain_at + 1 : gain_at + 2, :] = small_ref[taps_count + 2 : taps_count + 3, :]
    lines_grad_ref[gain_at + 2 : gain_at + 3, :] = small_ref[taps_count + 1 : taps_count + 2, :]
    lines_grad_ref[gain_at + 3 : gain_at + 4, :] = small_ref[taps_count : taps_count + 1, :]
    lines_grad_ref[gain_at + 4 : gain_at + 5, :] = gain_four_ref[0:1, :]
    out_ref[...] = lines_grad_ref[...].T.astype(BF)


def spec(kind):
    space = {"v": pltpu.VMEM, "s": pltpu.SMEM, "a": pl.ANY}[kind]
    return pl.BlockSpec(memory_space=space)


def shaped(shape, dtype):
    return jax.ShapeDtypeStruct(shape, dtype)


def call(kernel, name, kinds, args, outs, out_kinds, scratch=(), flops=0, moved=0):
    return pl.pallas_call(
        kernel,
        name=name,
        out_shape=tuple(outs),
        in_specs=[spec(kind) for kind in kinds],
        out_specs=tuple(spec(kind) for kind in out_kinds),
        scratch_shapes=list(scratch),
        compiler_params=pltpu.CompilerParams(vmem_limit_bytes=VMEM_BYTES),
        cost_estimate=pl.CostEstimate(flops=int(flops), bytes_accessed=int(moved), transcendentals=0),
    )(*args)


def ring_order(size):
    return list(range(0, size, 2)) + list(range(size - 1 - (size % 2), 0, -2))


def ring_pairs(size, experts):
    order = ring_order(size)
    pairs = []
    for place in range(size):
        for e in range(experts):
            step = 1 if e % 2 == 0 else -1
            pairs.append((order[place] * experts + e, order[(place + step) % size] * experts + e))
    return pairs


def rank_table(size):
    order = ring_order(size)
    where = {rank: place for place, rank in enumerate(order)}
    table = np.zeros((size, 2, size), np.int32)
    for rank in range(size):
        for core in range(2):
            step = 1 if core == 0 else -1
            for k in range(size):
                table[rank, core, k] = order[(where[rank] - step * k) % size]
    return table


def tie(value, *others):
    return lax.optimization_barrier((value, *others))[0]


def ring_step(array, pairs):
    return lax.ppermute(array, ALL, pairs)


def ring_gather(shard, pairs, size):
    chunks = [shard]
    for _ in range(size - 1):
        chunks.append(ring_step(chunks[-1], pairs))
    return chunks


def core_swap(array, experts):
    return lax.ppermute(array, "expert", [(e, e ^ 1) for e in range(experts)])


def over_chips(array, experts):
    total = array.astype(F32)
    chips = experts // 2
    for shift in range(1, chips):
        moved = lax.ppermute(
            array, "expert", [(e, (e // 2 + shift) % chips * 2 + e % 2) for e in range(experts)]
        )
        total = total + moved.astype(F32)
    return total


def swap_rows(slots, experts):
    parts = slots.reshape(experts, slots.shape[0] // experts, slots.shape[1])
    return lax.all_to_all(parts, "expert", split_axis=0, concat_axis=0, tiled=True).reshape(slots.shape)


def shared_finish(partial, experts, core):
    own = over_chips(partial, experts).astype(BF)
    far = core_swap(own, experts)
    return jnp.where(core == 0, jnp.concatenate([own, far], 1), jnp.concatenate([far, own], 1))


def shared_scatter(mine, other, pairs, size, experts, core):
    arrived = core_swap(other, experts)
    partial = (mine[0] + arrived[0]).astype(BF)
    for k in range(1, size):
        partial = ring_step(partial, pairs) + (mine[k] + arrived[k])
    return shared_finish(partial, experts, core)


def expert_scatter(chunks, pairs):
    partial = chunks[0]
    for chunk in chunks[1:]:
        partial = ring_step(partial, pairs) + chunk
    return partial


def adamw(gradient, master, moment, square, rate, decay):
    moment = BETA_ONE * moment + (1.0 - BETA_ONE) * gradient
    square = BETA_TWO * square + (1.0 - BETA_TWO) * gradient * gradient
    update = (
        moment / (1.0 - BETA_ONE**STEP) / (jnp.sqrt(square / (1.0 - BETA_TWO**STEP)) + ADAM_EPS)
    )
    return (moment, square, master - rate * (update + decay * master))


def on_device(features, lengths, routes, alignment, *weights):
    copies, masters, firsts, seconds = (weights[8 * i : 8 * i + 8] for i in range(4))
    attend_copy, output_copy, conv_copy, head_copy, extra_copy, gains_copy, up_copy, down_copy = copies
    size = lax.axis_size("dp")
    experts = lax.axis_size("expert")
    dp_at = lax.axis_index("dp")
    expert_at = lax.axis_index("expert")
    core = expert_at % 2
    row_count, feat_count = features.shape
    shard = attend_copy.shape[0]
    width = shard * size
    vocab = head_copy.shape[1]
    units = up_copy.shape[3]
    aux = extra_copy.shape[1]
    taps_count = aux - 2 * experts - feat_count
    tap_at = 2 * experts + feat_count
    gain_at = aux
    capacity = row_count * 5 // (4 * experts)
    slot_count = experts * capacity
    pairs = ring_pairs(size, experts)
    table = jnp.asarray(rank_table(size))[dp_at]
    ranks = jnp.concatenate(
        [
            lax.dynamic_index_in_dim(table, core, 0, keepdims=True),
            lax.dynamic_index_in_dim(table, 1 - core, 0, keepdims=True),
            jnp.full((1, size), core, jnp.int32),
        ]
    )

    everyone = size * experts
    gain_count = gains_copy.shape[0]
    frames_here = row_count - lengths[0, 3]
    digits = jnp.stack([frames_here // 16, frames_here % 16]).astype(BF)
    pack = jnp.concatenate(
        [
            extra_copy,
            gains_copy.T,
            jnp.broadcast_to(digits[None], (shard, 2)),
            jnp.zeros((shard, LANES - aux - gain_count - 2), BF),
        ],
        axis=1,
    )
    packs = lax.all_to_all(
        jnp.broadcast_to(pack[None], (size,) + pack.shape), "dp", split_axis=0, concat_axis=0, tiled=True
    )
    extra = packs.reshape(width, LANES)
    tops = jnp.sum(packs[:, 0].astype(F32), axis=0)
    frames = jnp.full((8, LANES), 16.0 * tops[gain_at + gain_count] + tops[gain_at + gain_count + 1])
    frames = frames + core_swap(frames, experts)
    frame_count = over_chips(frames, experts)[0, 0]

    expert_shards = [
        jnp.stack([up_copy[f, 0], down_copy[f, 0].T]) for f in range(2)
    ]
    second_chunks = ring_gather(expert_shards[1], pairs, size)
    shared = jnp.concatenate([attend_copy, output_copy, conv_copy], axis=1)
    half_shared = shared.shape[1] // 2
    shared_chunks = ring_gather(
        lax.dynamic_slice_in_dim(shared, core * half_shared, half_shared, 1), pairs, size
    )
    shared_mine = jnp.stack(shared_chunks)
    shared_other = core_swap(shared_mine, experts)
    half_vocab = vocab // 2
    head_half = lax.dynamic_slice_in_dim(head_copy, core * half_vocab, half_vocab, 1)

    square = (row_count, width)
    lanes = (row_count, LANES)
    cols, place_one, across_one, place_two, across_two = call(
        functools.partial(routing_kernel, capacity),
        "routing",
        "vv",
        (jnp.swapaxes(routes, 1, 2), alignment[None, :]),
        [shaped(lanes, F32)]
        + [shaped((slot_count, row_count), BF), shaped((row_count, slot_count), BF)] * 2,
        "vvvvv",
    )
    features_across = features.T

    def front(feat_ref, extra_ref, place_ref, *outs):
        front_kernel(experts, feat_ref, extra_ref, place_ref, gain_at, *outs)

    x0, slots_one, prob_one, lines = call(
        front,
        "front",
        "vvv",
        (features_across, extra, place_one),
        [shaped(square, F32), shaped((slot_count, width), BF), shaped(lanes, F32), shaped((LANES, width), F32)],
        "vvvv",
        flops=1e9,
        moved=4e6,
    )
    tile = 1024
    expert_scratch = [
        pltpu.VMEM((2, width, units), BF),
        pltpu.SemaphoreType.DMA((units // tile, size)),
    ]
    grads_scratch = [pltpu.VMEM((2, width, units), BF), pltpu.SemaphoreType.DMA((size,))]

    def expert_forward(slots, chunks):
        return call(
            functools.partial(expert_forward_kernel, size, tile),
            "expert_forward",
            "sv" + "a" * size,
            (ranks, slots, *chunks),
            [shaped(slots.shape, BF)],
            "v",
            expert_scratch,
            flops=4.0 * slot_count * width * units,
            moved=6e6,
        )[0]

    received_one = swap_rows(slots_one, experts)
    waits = {2: [extra], 4: [slots_one], 6: [received_one]}
    first_chunks = [expert_shards[0]]
    for k in range(1, size):
        first_chunks.append(ring_step(tie(first_chunks[-1], *waits.get(k, [])), pairs))
    head_mine = lax.all_gather(
        tie(head_half, first_chunks[-1], second_chunks[-1], shared_chunks[-1]), "dp", axis=0, tiled=True
    )
    returned_one = swap_rows(expert_forward(received_one, first_chunks), experts)
    copy_sems = pltpu.SemaphoreType.DMA((2 * size,))
    middle_dims = (experts, size, shard, tap_at, taps_count, gain_at)
    h1, h2, h3, logs, prob_two, slots_two, mixed, packed, blended = call(
        functools.partial(middle_forward_kernel, middle_dims),
        "middle_forward",
        "ssvvvvvvvvaa",
        (
            ranks,
            lengths,
            x0,
            prob_one,
            cols,
            across_one,
            returned_one,
            place_two,
            extra,
            lines,
            shared_mine,
            shared_other,
        ),
        [shaped(square, F32)] * 3
        + [
            shaped(lanes, F32),
            shaped(lanes, F32),
            shaped((slot_count, width), BF),
            shaped(square, F32),
            shaped((row_count, 3 * width), BF),
            shaped(square, BF),
        ],
        "vvvvvvvvv",
        [
            pltpu.VMEM((width, 7 * width), BF),
            pltpu.VMEM((row_count + 2 * TAP_PAD, width), F32),
            pltpu.VMEM(lanes, F32),
            copy_sems,
        ],
        flops=12e9,
        moved=10e6,
    )
    received_two = swap_rows(slots_two, experts)
    expert_two = expert_forward(received_two, second_chunks)
    returned_two = swap_rows(expert_two, experts)
    head_mine = tie(head_mine, expert_two)
    head_other = core_swap(head_mine, experts)
    two_grad, logit_two, grad_slots_two, gain_four, loss_part, head_grad_mine, head_grad_other = call(
        functools.partial(head_kernel, (experts, size, shard, gain_at, 2048)),
        "head",
        "sssvvvvvvvaa",
        (
            ranks,
            lengths,
            frame_count.reshape(1, 1),
            h3,
            prob_two,
            cols,
            across_two,
            returned_two,
            place_two,
            lines,
            head_mine,
            head_other,
        ),
        [
            shaped(square, F32),
            shaped(lanes, BF),
            shaped((slot_count, width), BF),
            shaped((8, width), F32),
            shaped((8, LANES), F32),
            shaped((width, half_vocab), BF),
            shaped((width, half_vocab), BF),
        ],
        "vvvvvaa",
        [
            pltpu.VMEM((width, vocab), BF),
            pltpu.VMEM((row_count, vocab), F32),
            pltpu.VMEM((width, vocab), BF),
            copy_sems,
        ],
        flops=20e9,
        moved=20e6,
    )

    def expert_backward(slots, grads, chunks):
        back, active, hidden = call(
            functools.partial(expert_backward_kernel, size, tile),
            "expert_backward",
            "svv" + "a" * size,
            (ranks, slots, grads, *chunks),
            [shaped(slots.shape, BF), shaped((slot_count, units), BF), shaped((slot_count, units), BF)],
            "vvv",
            expert_scratch,
            flops=6.0 * slot_count * width * units,
            moved=12e6,
        )
        sums = call(
            functools.partial(expert_grads_kernel, size, tile),
            "expert_grads",
            "svvvv",
            (ranks, slots, grads, active, hidden),
            [shaped((2, shard, units), BF)] * size,
            "a" * size,
            grads_scratch,
            flops=4.0 * slot_count * width * units,
            moved=10e6,
        )
        return back, sums

    head_total = head_grad_mine + core_swap(head_grad_other, experts)
    out_grad_two = tie(swap_rows(grad_slots_two, experts), head_total)
    head_part = lax.psum_scatter(head_total, "dp", scatter_dimension=0, tiled=True)
    back_two, sums_two = expert_backward(received_two, out_grad_two, second_chunks)
    slot_grad_two = tie(swap_rows(back_two, experts), sums_two[0])
    one_grad, logit_one, grad_slots_one, small, router_two, mid_grad_mine, mid_grad_other = call(
        functools.partial(middle_backward_kernel, middle_dims),
        "middle_backward",
        "ss" + "v" * 18 + "aa",
        (
            ranks,
            lengths,
            two_grad,
            slot_grad_two,
            across_two,
            logit_two,
            h1,
            h2,
            h3,
            logs,
            prob_one,
            cols,
            across_one,
            returned_one,
            place_one,
            extra,
            lines,
            mixed,
            packed,
            blended,
            shared_mine,
            shared_other,
        ),
        [
            shaped(square, F32),
            shaped(lanes, BF),
            shaped((slot_count, width), BF),
            shaped((24, width), F32),
            shaped((LANES, width), F32),
            shaped((size, shard, half_shared), BF),
            shaped((size, shard, half_shared), BF),
        ],
        "vvvvvaa",
        [
            pltpu.VMEM((width, 7 * width), BF),
            pltpu.VMEM((row_count, 3 * width), BF),
            pltpu.VMEM((row_count + 2 * TAP_PAD, width), F32),
            pltpu.VMEM((row_count + 2 * TAP_PAD, width), F32),
            pltpu.VMEM(lanes, F32),
            pltpu.VMEM(square, F32),
            pltpu.VMEM((16, 8, width), F32),
            pltpu.VMEM((width, 7 * width), BF),
            copy_sems,
        ],
        flops=25e9,
        moved=20e6,
    )
    out_grad_one = swap_rows(grad_slots_one, experts)
    back_one, sums_one = expert_backward(received_one, out_grad_one, first_chunks)
    slot_grad_one = tie(swap_rows(back_one, experts), sums_one[0])
    (extra_grad,) = call(
        functools.partial(back_kernel, (experts, tap_at, taps_count, gain_at)),
        "back",
        "v" * 11,
        (
            one_grad,
            slot_grad_one,
            across_one,
            logit_one,
            x0,
            features_across,
            extra,
            lines,
            small,
            router_two,
            gain_four,
        ),
        [shaped((width, LANES), BF)],
        "v",
        [pltpu.VMEM((LANES, width), F32)],
        flops=2e9,
        moved=5e6,
    )

    head_sum = shared_finish(head_part, experts, core).astype(F32)
    sums_two = expert_scatter(sums_two, pairs)
    mid_sum = shared_scatter(mid_grad_mine, mid_grad_other, pairs, size, experts, core).astype(F32)
    one_sum = sums_one[0]
    for k in range(1, size):
        one_sum = ring_step(tie(one_sum, *([head_sum] if k == 4 else [])), pairs) + sums_one[k]
    sums_one = one_sum
    spread = jnp.broadcast_to(
        extra_grad.reshape(size, 1, shard, LANES), (size, experts, shard, LANES)
    ).reshape(everyone, shard, LANES)
    small_sum = jnp.sum(
        lax.all_to_all(spread, ALL, split_axis=0, concat_axis=0, tiled=True).astype(F32), axis=0
    )
    extra_sum = small_sum[:, :aux]
    gains_sum = small_sum[:, aux : aux + gains_copy.shape[0]].T
    attend_sum = mid_sum[:, : 3 * width]
    output_sum = mid_sum[:, 3 * width : 4 * width]
    conv_sum = mid_sum[:, 4 * width :]
    up_sum = jnp.stack([sums_one[0], sums_two[0]])[:, None].astype(F32)
    down_sum = jnp.stack([sums_one[1], sums_two[1]])[:, None].astype(F32)
    shared_squares = jnp.float32(0.0)
    for member in (mid_sum, head_sum, extra_sum, gains_sum):
        shared_squares = shared_squares + jnp.sum(member * member)
    expert_squares = jnp.sum(up_sum * up_sum) + jnp.sum(down_sum * down_sum)
    local_squares = jnp.where(expert_at == 0, shared_squares, 0.0) + expert_squares
    totals = jnp.stack([local_squares, loss_part[0, 0]])
    totals = jnp.sum(
        lax.all_to_all(
            jnp.broadcast_to(totals[None, :, None], (everyone, 2, LANES)),
            ALL,
            split_axis=0,
            concat_axis=0,
            tiled=True,
        )[:, :, 0],
        axis=0,
    )
    global_norm = jnp.sqrt(totals[0])
    loss_sum = totals[1]
    factor = jnp.minimum(1.0, 0.1 * math.sqrt(width / (row_count * everyone)) / global_norm)
    gradients = (attend_sum, output_sum, conv_sum, head_sum, extra_sum, gains_sum, up_sum, down_sum)
    turned = lambda arrays: arrays[:7] + (jnp.swapaxes(arrays[7], 2, 3),)
    results = [
        adamw(gradient * factor, master, moment, second, rate, decay)
        for gradient, master, moment, second, rate, decay in zip(
            gradients, turned(masters), turned(firsts), turned(seconds), STEP_RATES, DECAYS
        )
    ]
    results[7] = tuple(jnp.swapaxes(member, 2, 3) for member in results[7])
    return (
        loss_sum,
        frame_count,
        global_norm,
        *(result[0] for result in results),
        *(result[1] for result in results),
        *(result[2] for result in results),
    )


def solution(mesh):
    weight_specs = (
        P("dp", None),
        P("dp", None),
        P("dp", None),
        P("dp", None),
        P("dp", None),
        P(None, "dp"),
        P(None, "expert", "dp", None),
        P(None, "expert", None, "dp"),
    )
    return jax.shard_map(
        on_device,
        mesh=mesh,
        in_specs=(
            P(("dp", "expert"), None),
            P(("dp", "expert"), None),
            P(None, ("dp", "expert"), None),
            P(("dp", "expert")),
        )
        + weight_specs * 4,
        out_specs=(P(), P(), P()) + weight_specs * 3,
        check_vma=False,
    )
```
